512 devices in a mesh: scan: 32 (over z, x), tile: 16 (over y, core).
Axes of the slice: x: 4, y: 8, z: 8, core: 2. Of those that a mesh axis runs over, the one named last changes fastest.
Arguments:
- object_field: float32 [2, 512, 6144], P(None, None, 'tile'), may hold values from -6 to 6
- probe: bfloat16 [3, 2, 128, 128], replicated, may hold values from -3 to 3
- measured: float32 [4096, 128, 128], P(('scan', 'tile')), may hold values from 0 to 12
- positions: int32 [4096, 2], P(('scan', 'tile')), may hold values from 0 to 5759, as said below
Outputs:
- object_grad: float32 [2, 512, 6144], P(None, 'scan', 'tile')
- probe_grad: float32 [3, 2, 128, 128], replicated
- position_grad: float32 [4096, 2], P(('scan', 'tile'))
The draws below stay inside these ranges and needn't reach their ends.
Inputs may be any that keep to these rules, and one draw needn't show every extreme that they name: `positions`: each column offset lies 1 to 127 columns left of the boundary between tiles k and k + 1 of 384 columns each (0 <= k <= 14), so every window covers columns of exactly two adjacent tiles; the 8 patterns of one device have different k; in every draw some k is taken by a pattern of every device of one group along tile; row offsets are at most 384.
All inputs are finite; a program needn't handle non-finite values.
Results may differ from the reference program's by a relative error of at most 0.003.
Values may be sent and summed in bfloat16 or wider, within the bound.
No kernel may reach another device: no remote copies, remote signals or barrier semaphores. Data moves between devices by JAX's collectives and lax.ppermute only.
A program may use at most 128 MiB of HBM per device.

```python
import jax
import jax.numpy as jnp
from jax import lax

WIN = 128
MODES = 3
TH = 512
TW = 384
P_DEV = 8
PATTERNS = 4096
OBJ_COLS = 6144
N_TILE = 16


def draw_positions(key, part):
    key = jax.random.fold_in(key, 7)
    subkeys = jax.random.split(key, 5)
    devices = PATTERNS // P_DEV
    left_count = N_TILE - 1
    random_jitter = jax.random.randint(subkeys[0], (devices, left_count), 0, 1000)
    sorted_order = jax.random.permutation(subkeys[1], left_count)
    priority_extra = jnp.where(sorted_order < 3, 600, 0)
    full_tile = jax.random.randint(subkeys[2], (), 0, left_count)
    tile_numbers = jnp.arange(left_count, dtype=jnp.int32)
    device_ids = jnp.arange(devices, dtype=jnp.int32)
    mandatory_pick = (device_ids[:, None] < N_TILE) & (tile_numbers[None, :] == full_tile)
    edge_devices = (device_ids >= N_TILE) & (device_ids < 2 * N_TILE)
    border_flag = edge_devices[:, None] & (tile_numbers[None, :] == left_count - 1)
    tile_scores = (random_jitter + priority_extra[None, :] + jnp.where(mandatory_pick | border_flag, 100000, 0)) * 64 + tile_numbers[None, :]
    chosen = lax.top_k(tile_scores, P_DEV)[1]
    left_tiles = chosen.reshape(PATTERNS).astype(jnp.int32)
    pattern_ids = jnp.arange(PATTERNS, dtype=jnp.int32)
    on_edge = edge_devices[pattern_ids // P_DEV] & (left_tiles == left_count - 1)
    inset = jax.random.randint(subkeys[3], (PATTERNS,), 1, WIN)
    inset = jnp.where(on_edge, 1, inset)
    column_offsets = (left_tiles + 1) * TW - inset
    row_offsets = jax.random.randint(subkeys[4], (PATTERNS,), 0, TH - WIN + 1)
    row_offsets = row_offsets.at[0].set(0)
    return jnp.stack([row_offsets, column_offsets], axis=1).astype(jnp.int32)


def levels(own_key, extent, shards, low, high):
    loudness = 1.0
    for axis_at, parts in shards:
        steps = jax.random.uniform(jax.random.fold_in(jax.random.fold_in(own_key, 6), axis_at), (parts,), jnp.float32, low / len(shards), high / len(shards))
        loudness = loudness * jnp.repeat(jnp.exp(steps), extent[axis_at] // parts).reshape((-1,) + (1,) * (len(extent) - 1 - axis_at))
    return loudness


def gaussian(stream_key, shape, spread, reach, cuts=(), kind=jnp.bfloat16):
    result = jax.random.normal(stream_key, shape, jnp.float32) * spread
    if len(cuts) > 0:
        result = levels(stream_key, shape, cuts, -0.22, 0.18) * result
    return jnp.clip(result, min=-reach, max=reach).astype(kind)


def setup_inputs(seed: int = 0) -> dict:
    key_list = jax.random.split(jax.random.key(seed), 5)
    return {
        "object_field": gaussian(key_list[0], (2, TH, OBJ_COLS), 1.0, 6.0, ((2, 16),), jnp.float32),
        "probe": gaussian(key_list[1], (MODES, 2, WIN, WIN), 0.5, 3.0),
        "measured": jnp.clip(12.0 * jax.random.uniform(key_list[2], (PATTERNS, WIN, WIN), jnp.float32) ** levels(key_list[2], (PATTERNS, WIN, WIN), ((0, 512),), -0.2, 0.2), 0.0, 12.0),
        "positions": draw_positions(jax.random.fold_in(key_list[4], 71), 0),
    }


def reference(object_field, probe, measured, positions):
    probe_complex = probe[:, 0].astype(jnp.float32) + 1j * probe[:, 1].astype(jnp.float32)
    anchor = jnp.zeros((), jnp.int32)

    def advance(running, element):
        accumulated, probe_running = running
        intensity, offset = element
        row_start = offset[0].astype(jnp.int32)
        column_start = offset[1].astype(jnp.int32)
        window = lax.dynamic_slice(object_field, (anchor, row_start, column_start), (2, WIN, WIN))
        window = lax.optimization_barrier(window.astype(jnp.bfloat16)).astype(jnp.float32)
        window_complex = window[0] + 1j * window[1]
        far_field = jnp.fft.fft2(probe_complex * window_complex[None], norm='ortho')
        modeled = lax.optimization_barrier(jnp.sum(far_field.real ** 2 + far_field.imag ** 2, axis=0))
        scaling = 1.0 - jnp.sqrt(intensity) / jnp.maximum(jnp.sqrt(modeled), 0.5)
        back_field = jnp.fft.ifft2(scaling[None] * far_field, norm='ortho')
        patch = lax.optimization_barrier(jnp.sum(jnp.conj(probe_complex) * back_field, axis=0))
        patch = jnp.stack([patch.real, patch.imag]).astype(jnp.bfloat16)
        patch = lax.optimization_barrier(patch).astype(accumulated.dtype)
        corner = (anchor, row_start, column_start)
        current = lax.dynamic_slice(accumulated, corner, (2, WIN, WIN))
        accumulated = lax.dynamic_update_slice(accumulated, current + patch, corner)
        probe_term = jnp.conj(window_complex)[None] * back_field
        probe_running = probe_running + jnp.stack([probe_term.real, probe_term.imag], axis=1)
        row_change = jnp.concatenate([window_complex[1:] - window_complex[:-1], jnp.zeros((1, WIN), window_complex.dtype)], axis=0)
        column_change = jnp.concatenate([window_complex[:, 1:] - window_complex[:, :-1], jnp.zeros((WIN, 1), window_complex.dtype)], axis=1)
        weighted = jnp.conj(back_field) * probe_complex
        position_grad = jnp.stack([jnp.sum((weighted * row_change[None]).real), jnp.sum((weighted * column_change[None]).real)]) / WIN
        return ((accumulated, probe_running), position_grad)
    start_state = (jnp.zeros((2, TH, OBJ_COLS), jnp.float32), jnp.zeros((MODES, 2, WIN, WIN), jnp.float32))
    (object_grad, probe_running), position_grad = lax.scan(advance, start_state, (measured, positions))
    probe_grad = probe_running / jnp.sqrt(jnp.float32(PATTERNS))
    return (object_grad, probe_grad, position_grad.astype(jnp.float32))
```

```python
import math

import jax
import jax.numpy as jnp
import numpy as np
from jax import lax
from jax.experimental import pallas as pl
from jax.experimental.pallas import tpu as pltpu
from jax.sharding import PartitionSpec as P

F32 = jnp.float32
BF16 = jnp.bfloat16
TOP = math.sqrt(12.0)
STEPS = 65535.0
HALF = 32768.0


def dft_tables(window):
    ramp = np.arange(window)
    angles = (ramp[:, None] * ramp[None, :] % window) * (2.0 * np.pi / window)
    cosine = np.cos(angles) / np.sqrt(window)
    sine = np.sin(angles) / np.sqrt(window)
    first = np.block([[cosine, -sine], [sine, cosine]])
    second = np.block([[cosine, sine], [-sine, cosine]])
    tables = []
    for table in (first, second):
        high = table.astype(np.float32).astype(BF16)
        low = (table - high.astype(np.float64)).astype(np.float32).astype(BF16)
        tables.append(np.concatenate([high, high, low], axis=0))
        tables.append(np.concatenate([high, high, low], axis=1))
    return tables


def split(value):
    high = value.astype(BF16)
    return high, (value - high.astype(F32)).astype(BF16)


def from_right(value, table):
    high, low = split(value)
    return jnp.dot(
        jnp.concatenate([high, low, high], axis=1), table, preferred_element_type=F32
    )


def from_left(table, value):
    high, low = split(value)
    return jnp.dot(
        table, jnp.concatenate([high, low, high], axis=0), preferred_element_type=F32
    )


def pack_kernel(positions, measured, packed):
    patterns = measured.shape[0]
    slots, rows, window = packed.shape
    packed[...] = jnp.zeros(packed.shape, jnp.int16)
    lane = lax.broadcasted_iota(jnp.int32, (rows - window, window), 1)
    for p in range(patterns):
        row = positions[p, 0]
        column = positions[p, 1]
        tile = column // (3 * window)
        start = column - tile * (3 * window) - 2 * window
        amplitude = jnp.sqrt(measured[p]) * (STEPS / TOP)
        level = jnp.clip(jnp.round(amplitude) - HALF, -HALF, HALF - 1.0)
        packed[tile, 0:window, :] = level.astype(jnp.int32).astype(jnp.int16)
        note = jnp.where(lane == 0, row, jnp.where(lane == 1, start, jnp.where(lane == 2, 1, 0)))
        packed[tile, window:rows, :] = note.astype(jnp.int16)


def main_kernel(
    notes, received, own, margin, probe, first_down, first_across, second_down, second_across,
    sums, shifts, strip, total, probe_total, probe_full,
):
    slots = received.shape[0]
    modes = probe.shape[0]
    window = probe.shape[2]
    bands = sums.shape[0]
    height = own.shape[1]
    for part in range(2):
        strip[part, 0] = own[part].astype(BF16).astype(F32)
        strip[part, 1] = margin[part].astype(F32)
        for m in range(modes):
            probe_full[m, part] = probe[m, part].astype(F32)
    total[...] = jnp.zeros(total.shape, F32)
    probe_total[...] = jnp.zeros(probe_total.shape, F32)
    lane = lax.broadcasted_iota(jnp.int32, (window, window), 1)
    row = lax.broadcasted_iota(jnp.int32, (window, window), 0)

    def one(slot):
        start_row = notes[slot, 0]
        start = jnp.clip(notes[slot, 1], 1, window - 1)
        valid = notes[slot, 2].astype(F32)
        rows = pl.ds(start_row, window)
        cut = []
        for part in range(2):
            near = pltpu.roll(strip[part, 0, rows, :], window - start, 1)
            far = pltpu.roll(strip[part, 1, rows, :], window - start, 1)
            cut.append(jnp.where(lane < window - start, near, far))
        w_re, w_im = cut
        exits = []
        for m in range(modes):
            p_re, p_im = probe_full[m, 0], probe_full[m, 1]
            exits.append(
                jnp.concatenate([p_re * w_re - p_im * w_im, p_re * w_im + p_im * w_re], axis=1)
            )
        half = from_right(jnp.concatenate(exits, axis=0), first_down[...])
        stacked = jnp.concatenate(
            [
                jnp.concatenate(
                    [half[m * window:(m + 1) * window, c * window:(c + 1) * window] for m in range(modes)],
                    axis=1,
                )
                for c in range(2)
            ],
            axis=0,
        )
        field = from_left(second_across[...], stacked)
        power = jnp.zeros((window, window), F32)
        for m in range(modes):
            for c in range(2):
                piece = field[c * window:(c + 1) * window, m * window:(m + 1) * window]
                power = power + piece * piece
        amplitude = (received[slot, 0:window, :].astype(jnp.int32).astype(F32) + HALF) * (TOP / STEPS)
        scaling = valid * (1.0 - amplitude * lax.rsqrt(jnp.maximum(power, 0.25)))
        scaled = jnp.concatenate(
            [
                jnp.concatenate(
                    [
                        scaling * field[c * window:(c + 1) * window, m * window:(m + 1) * window]
                        for c in range(2)
                    ],
                    axis=1,
                )
                for m in range(modes)
            ],
            axis=0,
        )
        half = from_right(scaled, second_down[...])
        stacked = jnp.concatenate(
            [
                jnp.concatenate(
                    [half[m * window:(m + 1) * window, c * window:(c + 1) * window] for m in range(modes)],
                    axis=1,
                )
                for c in range(2)
            ],
            axis=0,
        )
        back = from_left(first_across[...], stacked)
        patch_re = jnp.zeros((window, window), F32)
        patch_im = jnp.zeros((window, window), F32)
        for m in range(modes):
            p_re, p_im = probe_full[m, 0], probe_full[m, 1]
            b_re = back[0:window, m * window:(m + 1) * window]
            b_im = back[window:, m * window:(m + 1) * window]
            patch_re = patch_re + (p_re * b_re + p_im * b_im)
            patch_im = patch_im + (p_re * b_im - p_im * b_re)
            probe_total[2 * m] += w_re * b_re + w_im * b_im
            probe_total[2 * m + 1] += w_re * b_im - w_im * b_re
        for axis, at in ((0, row), (1, lane)):
            change = patch_re * (pltpu.roll(w_re, window - 1, axis) - w_re) + patch_im * (
                pltpu.roll(w_im, window - 1, axis) - w_im
            )
            change = jnp.where(at < window - 1, change, 0.0)
            shifts[slot, pl.ds(axis, 1), :] = jnp.sum(change, axis=0, keepdims=True)
        for part, patch in enumerate((patch_re, patch_im)):
            turned = pltpu.roll(patch.astype(BF16).astype(F32), start, 1)
            total[part, 0, rows, :] += jnp.where(lane >= start, turned, 0.0)
            total[part, 1, rows, :] += jnp.where(lane < start, turned, 0.0)

    def step(at, carry):
        one(at)
        return carry

    shifts[...] = jnp.zeros(shifts.shape, F32)
    lax.fori_loop(0, slots, step, 0)
    deep = height // bands
    piece = 2 * modes * window // bands
    for b in range(bands):
        for part in range(2):
            for side in range(2):
                at = (2 * part + side) * deep
                sums[b, at:at + deep, :] = total[part, side, b * deep:(b + 1) * deep, :].astype(BF16)
        mode, offset = divmod(b * piece, window)
        parts = []
        left = piece
        while left:
            take = min(left, window - offset)
            parts.append(probe_total[mode, offset:offset + take, :])
            mode, offset, left = mode + 1, 0, left - take
        parts.append(jnp.zeros((sums.shape[1] - 4 * deep - piece, window), F32))
        sums[b, 4 * deep:, :] = jnp.concatenate(parts, axis=0).astype(BF16)


def pack(positions, measured, slots):
    window = measured.shape[2]
    return pl.pallas_call(
        pack_kernel,
        out_shape=jax.ShapeDtypeStruct((slots, window + 16, window), jnp.int16),
        in_specs=[
            pl.BlockSpec(memory_space=pltpu.SMEM),
            pl.BlockSpec(memory_space=pltpu.VMEM),
        ],
        out_specs=pl.BlockSpec(memory_space=pltpu.VMEM),
        compiler_params=pltpu.CompilerParams(vmem_limit_bytes=16 * 2**20),
    )(positions, measured)


def compute(notes, received, object_field, margin, probe, bands):
    modes, window = probe.shape[0], probe.shape[2]
    slots = received.shape[0]
    height = object_field.shape[1]
    tables = [jnp.asarray(table) for table in dft_tables(window)]
    vmem = pl.BlockSpec(memory_space=pltpu.VMEM)

    def whole(shape):
        return pl.BlockSpec(shape, lambda i: (0,) * len(shape))

    rows = 4 * (height // bands) + -(-(2 * modes * window // bands) // 16) * 16
    return pl.pallas_call(
        main_kernel,
        grid=(1,),
        out_shape=(
            jax.ShapeDtypeStruct((bands, rows, window), BF16),
            jax.ShapeDtypeStruct((slots, 8, window), F32),
        ),
        in_specs=[
            pl.BlockSpec(memory_space=pltpu.SMEM),
            whole(received.shape),
            pl.BlockSpec((2, height, window), lambda i: (0, 0, 2)),
            whole(margin.shape),
            whole(probe.shape),
        ] + [whole(table.shape) for table in tables],
        out_specs=(whole((bands, rows, window)), whole((slots, 8, window))),
        scratch_shapes=[
            pltpu.VMEM((2, 2, height, window), F32),
            pltpu.VMEM((2, 2, height, window), F32),
            pltpu.VMEM((2 * modes, window, window), F32),
            pltpu.VMEM((modes, 2, window, window), F32),
        ],
        compiler_params=pltpu.CompilerParams(vmem_limit_bytes=40 * 2**20),
    )(notes, received, object_field, margin, probe, *tables)


def exchange(value, axis):
    return lax.all_to_all(value, axis, split_axis=0, concat_axis=0, tiled=True)


def local(object_field, probe, measured, positions):
    tiles = lax.axis_size("tile")
    bands = lax.axis_size("scan")
    width = object_field.shape[2]
    height = object_field.shape[1]
    modes, window = probe.shape[0], probe.shape[2]
    patterns = measured.shape[0]
    deep = height // bands
    piece = 2 * modes * window // bands
    margin = lax.ppermute(
        object_field[:, :, :window].astype(BF16), "tile", [(t, t - 1) for t in range(1, tiles)]
    )
    received = exchange(pack(positions, measured, tiles), "tile")
    notes = received[:, window, :3].astype(jnp.int32)
    sums, shifts = compute(notes, received, object_field, margin, probe, bands)
    gathered = jnp.sum(exchange(sums, "scan").astype(F32), axis=0)
    strips = gathered[:4 * deep].reshape(2, 2, deep, window)
    spilled = lax.ppermute(strips[:, 1], "tile", [(t, t + 1) for t in range(tiles - 1)])
    object_grad = jnp.concatenate(
        [spilled, jnp.zeros((2, deep, width - 2 * window), F32), strips[:, 0]], axis=2
    )
    own_piece = gathered[4 * deep:4 * deep + piece]
    outgoing = jnp.concatenate(
        [jnp.broadcast_to(own_piece[None], (tiles, piece, window)), shifts], axis=1
    )
    mixed = exchange(outgoing, "tile")
    full_piece = jnp.sum(mixed[:, :piece], axis=0) / math.sqrt(patterns * bands * tiles)
    probe_grad = exchange(
        jnp.broadcast_to(full_piece[None], (bands, piece, window)), "scan"
    ).reshape(modes, 2, window, window)
    per_tile = jnp.sum(mixed[:, piece:piece + 2], axis=2) / window
    left_tile = positions[:, 1] // width
    hits = left_tile[:, None] == jnp.arange(tiles, dtype=jnp.int32)[None, :]
    position_grad = jnp.sum(jnp.where(hits[:, :, None], per_tile[None], 0.0), axis=1)
    return (object_grad, probe_grad, position_grad)


def solution(mesh):
    return jax.shard_map(
        local,
        mesh=mesh,
        in_specs=(
            P(None, None, "tile"),
            P(),
            P(("scan", "tile"), None, None),
            P(("scan", "tile"), None),
        ),
        out_specs=(P(None, "scan", "tile"), P(), P(("scan", "tile"), None)),
        check_vma=False,
    )
```

```python
import math

import jax
import jax.numpy as jnp
import numpy as np
from jax import lax
from jax.experimental import pallas as pl
from jax.experimental.pallas import tpu as pltpu
from jax.sharding import PartitionSpec as P

F32 = jnp.float32
BF16 = jnp.bfloat16
TOP = math.sqrt(12.0)
STEPS = 65535.0
HALF = 32768.0
GROUP = 16


def dft_tables(window):
    ramp = np.arange(window)
    angles = (ramp[:, None] * ramp[None, :] % window) * (2.0 * np.pi / window)
    cosine = np.cos(angles) / np.sqrt(window)
    sine = np.sin(angles) / np.sqrt(window)
    first = np.block([[cosine, -sine], [sine, cosine]])
    second = np.block([[cosine, sine], [-sine, cosine]])
    tables = []
    for table in (first, second):
        high = table.astype(np.float32).astype(BF16)
        low = (table - high.astype(np.float64)).astype(np.float32).astype(BF16)
        tables.append(np.concatenate([high, low], axis=0))
        tables.append(np.concatenate([high, low], axis=1))
    return tables


def split(value):
    high = value.astype(BF16)
    return high, (value - high.astype(F32)).astype(BF16)


def from_right(value, table):
    high = value.astype(BF16)
    return jnp.dot(jnp.concatenate([high, high], axis=1), table, preferred_element_type=F32)


def from_left(table, value):
    high = value.astype(BF16)
    return jnp.dot(table, jnp.concatenate([high, high], axis=0), preferred_element_type=F32)


def pack_kernel(positions, measured, packed):
    patterns = measured.shape[0]
    slots, rows, window = packed.shape
    packed[...] = jnp.zeros(packed.shape, jnp.int16)
    lane = lax.broadcasted_iota(jnp.int32, (rows - window, window), 1)
    for p in range(patterns):
        row = positions[p, 0]
        column = positions[p, 1]
        tile = column // (3 * window)
        start = column - tile * (3 * window) - 2 * window
        amplitude = jnp.sqrt(measured[p]) * (STEPS / TOP)
        level = jnp.clip(jnp.round(amplitude) - HALF, -HALF, HALF - 1.0)
        packed[tile, 0:window, :] = level.astype(jnp.int32).astype(jnp.int16)
        note = jnp.where(lane == 0, row, jnp.where(lane == 1, start, jnp.where(lane == 2, 1, 0)))
        packed[tile, window:rows, :] = note.astype(jnp.int16)


def main_kernel(
    notes, received, own, margin, probe, first_down, first_across, second_down, second_across,
    sums, shifts, strip, total, probe_total, probe_full,
):
    slots = received.shape[0]
    modes = probe.shape[0]
    window = probe.shape[2]
    bands = sums.shape[0]
    height = own.shape[1]
    for part in range(2):
        strip[part, 0] = own[part].astype(BF16).astype(F32)
        strip[part, 1] = margin[part].astype(F32)
        for m in range(modes):
            probe_full[m, part] = probe[m, part].astype(F32)
    total[...] = jnp.zeros(total.shape, F32)
    probe_total[...] = jnp.zeros(probe_total.shape, F32)
    lane = lax.broadcasted_iota(jnp.int32, (window, window), 1)
    row = lax.broadcasted_iota(jnp.int32, (window, window), 0)

    def cut(slot):
        start = jnp.clip(notes[slot, 1], 1, window - 1)
        rows = pl.ds(notes[slot, 0], window)
        both = []
        for part in range(2):
            near = pltpu.roll(strip[part, 0, rows, :], window - start, 1)
            far = pltpu.roll(strip[part, 1, rows, :], window - start, 1)
            both.append(jnp.where(lane < window - start, near, far))
        return both

    def leave(w_re, w_im):
        exits = []
        for m in range(modes):
            p_re, p_im = probe_full[m, 0], probe_full[m, 1]
            exits.append(
                jnp.concatenate([p_re * w_re - p_im * w_im, p_re * w_im + p_im * w_re], axis=1)
            )
        return exits

    def scale_of(slot, blocks):
        power = blocks[0][0] * blocks[0][0]
        for m in range(modes):
            for c in range(2):
                if m or c:
                    power = power + blocks[m][c] * blocks[m][c]
        amplitude = (received[slot, 0:window, :].astype(jnp.int32).astype(F32) + HALF) * (TOP / STEPS)
        return notes[slot, 2].astype(F32) * (1.0 - amplitude * lax.rsqrt(jnp.maximum(power, 0.25)))

    def finish(slot, w_re, w_im, back):
        start = jnp.clip(notes[slot, 1], 1, window - 1)
        rows = pl.ds(notes[slot, 0], window)
        patch_re = jnp.zeros((window, window), F32)
        patch_im = jnp.zeros((window, window), F32)
        for m in range(modes):
            p_re, p_im = probe_full[m, 0], probe_full[m, 1]
            b_re, b_im = back[m]
            patch_re = patch_re + (p_re * b_re + p_im * b_im)
            patch_im = patch_im + (p_re * b_im - p_im * b_re)
            probe_total[2 * m] += w_re * b_re + w_im * b_im
            probe_total[2 * m + 1] += w_re * b_im - w_im * b_re
        for axis, at in ((0, row), (1, lane)):
            change = patch_re * (pltpu.roll(w_re, window - 1, axis) - w_re) + patch_im * (
                pltpu.roll(w_im, window - 1, axis) - w_im
            )
            change = jnp.where(at < window - 1, change, 0.0)
            shifts[slot, pl.ds(axis, 1), :] = jnp.sum(change, axis=0, keepdims=True)
        for part, patch in enumerate((patch_re, patch_im)):
            turned = pltpu.roll(patch.astype(BF16).astype(F32), start, 1)
            total[part, 0, rows, :] += jnp.where(lane >= start, turned, 0.0)
            total[part, 1, rows, :] += jnp.where(lane < start, turned, 0.0)

    def several(slots_now):
        cuts = [cut(slot) for slot in slots_now]
        exits = [e for w in cuts for e in leave(*w)]
        field = both_ways(exits, first_down[...], second_across[...])
        scaled = []
        for u, slot in enumerate(slots_now):
            mine = field[u * modes:(u + 1) * modes]
            scaling = scale_of(slot, mine)
            scaled += [jnp.concatenate([scaling * b[0], scaling * b[1]], axis=1) for b in mine]
        back = both_ways(scaled, second_down[...], first_across[...])
        for u, slot in enumerate(slots_now):
            finish(slot, *cuts[u], back[u * modes:(u + 1) * modes])

    def both_ways(blocks, down, across):
        count = len(blocks)
        half = from_right(jnp.concatenate(blocks, axis=0), down)
        pieces = [
            [half[b * window:(b + 1) * window, c * window:(c + 1) * window] for c in range(2)]
            for b in range(count)
        ]
        stacked = jnp.concatenate(
            [jnp.concatenate([p[c] for p in pieces], axis=1) for c in range(2)], axis=0
        )
        out = from_left(across, stacked)
        return [
            [out[c * window:(c + 1) * window, b * window:(b + 1) * window] for c in range(2)]
            for b in range(count)
        ]

    def step(at, carry):
        several([GROUP * at + u for u in range(GROUP)])
        return carry

    shifts[...] = jnp.zeros(shifts.shape, F32)
    lax.fori_loop(0, slots // GROUP, step, 0)
    deep = height // bands
    piece = 2 * modes * window // bands
    for b in range(bands):
        for part in range(2):
            for side in range(2):
                at = (2 * part + side) * deep
                sums[b, at:at + deep, :] = total[part, side, b * deep:(b + 1) * deep, :].astype(BF16)
        mode, offset = divmod(b * piece, window)
        parts = []
        left = piece
        while left:
            take = min(left, window - offset)
            parts.append(probe_total[mode, offset:offset + take, :])
            mode, offset, left = mode + 1, 0, left - take
        parts.append(jnp.zeros((sums.shape[1] - 4 * deep - piece, window), F32))
        sums[b, 4 * deep:, :] = jnp.concatenate(parts, axis=0).astype(BF16)


def pack(positions, measured, slots):
    window = measured.shape[2]
    return pl.pallas_call(
        pack_kernel,
        out_shape=jax.ShapeDtypeStruct((slots, window + 16, window), jnp.int16),
        in_specs=[
            pl.BlockSpec(memory_space=pltpu.SMEM),
            pl.BlockSpec(memory_space=pltpu.VMEM),
        ],
        out_specs=pl.BlockSpec(memory_space=pltpu.VMEM),
        compiler_params=pltpu.CompilerParams(vmem_limit_bytes=16 * 2**20),
    )(positions, measured)


def compute(notes, received, object_field, margin, probe, bands):
    modes, window = probe.shape[0], probe.shape[2]
    slots = received.shape[0]
    height = object_field.shape[1]
    tables = [jnp.asarray(table) for table in dft_tables(window)]
    vmem = pl.BlockSpec(memory_space=pltpu.VMEM)

    def whole(shape):
        return pl.BlockSpec(shape, lambda i: (0,) * len(shape))

    rows = 4 * (height // bands) + -(-(2 * modes * window // bands) // 16) * 16
    return pl.pallas_call(
        main_kernel,
        grid=(1,),
        out_shape=(
            jax.ShapeDtypeStruct((bands, rows, window), BF16),
            jax.ShapeDtypeStruct((slots, 8, window), F32),
        ),
        in_specs=[
            pl.BlockSpec(memory_space=pltpu.SMEM),
            whole(received.shape),
            pl.BlockSpec((2, height, window), lambda i: (0, 0, 2)),
            whole(margin.shape),
            whole(probe.shape),
        ] + [whole(table.shape) for table in tables],
        out_specs=(whole((bands, rows, window)), whole((slots, 8, window))),
        scratch_shapes=[
            pltpu.VMEM((2, 2, height, window), F32),
            pltpu.VMEM((2, 2, height, window), F32),
            pltpu.VMEM((2 * modes, window, window), F32),
            pltpu.VMEM((modes, 2, window, window), F32),
        ],
        compiler_params=pltpu.CompilerParams(vmem_limit_bytes=40 * 2**20),
    )(notes, received, object_field, margin, probe, *tables)


def exchange(value, axis):
    return lax.all_to_all(value, axis, split_axis=0, concat_axis=0, tiled=True)


def local(object_field, probe, measured, positions):
    tiles = lax.axis_size("tile")
    bands = lax.axis_size("scan")
    width = object_field.shape[2]
    height = object_field.shape[1]
    modes, window = probe.shape[0], probe.shape[2]
    patterns = measured.shape[0]
    deep = height // bands
    piece = 2 * modes * window // bands
    margin = lax.ppermute(
        object_field[:, :, :window].astype(BF16), "tile", [(t, t - 1) for t in range(1, tiles)]
    )
    received = exchange(pack(positions, measured, tiles), "tile")
    notes = received[:, window, :3].astype(jnp.int32)
    sums, shifts = compute(notes, received, object_field, margin, probe, bands)
    gathered = jnp.sum(exchange(sums, "scan").astype(F32), axis=0)
    strips = gathered[:4 * deep].reshape(2, 2, deep, window)
    spilled = lax.ppermute(strips[:, 1], "tile", [(t, t + 1) for t in range(tiles - 1)])
    object_grad = jnp.concatenate(
        [spilled, jnp.zeros((2, deep, width - 2 * window), F32), strips[:, 0]], axis=2
    )
    own_piece = gathered[4 * deep:4 * deep + piece]
    outgoing = jnp.concatenate(
        [jnp.broadcast_to(own_piece[None], (tiles, piece, window)), shifts], axis=1
    )
    mixed = exchange(outgoing, "tile")
    full_piece = jnp.sum(mixed[:, :piece], axis=0) / math.sqrt(patterns * bands * tiles)
    probe_grad = exchange(
        jnp.broadcast_to(full_piece[None], (bands, piece, window)), "scan"
    ).reshape(modes, 2, window, window)
    per_tile = jnp.sum(mixed[:, piece:piece + 2], axis=2) / window
    left_tile = positions[:, 1] // width
    hits = left_tile[:, None] == jnp.arange(tiles, dtype=jnp.int32)[None, :]
    position_grad = jnp.sum(jnp.where(hits[:, :, None], per_tile[None], 0.0), axis=1)
    return (object_grad, probe_grad, position_grad)


def solution(mesh):
    return jax.shard_map(
        local,
        mesh=mesh,
        in_specs=(
            P(None, None, "tile"),
            P(),
            P(("scan", "tile"), None, None),
            P(("scan", "tile"), None),
        ),
        out_specs=(P(None, "scan", "tile"), P(), P(("scan", "tile"), None)),
        check_vma=False,
    )
```

```python
import math

import jax
import jax.numpy as jnp
import numpy as np
from jax import lax
from jax.experimental import pallas as pl
from jax.experimental.pallas import tpu as pltpu
from jax.sharding import PartitionSpec as P

F32 = jnp.float32
BF16 = jnp.bfloat16
TOP = math.sqrt(12.0)
STEPS = 65535.0
HALF = 32768.0
GROUP = 16


def dft_tables(window):
    ramp = np.arange(window)
    angles = (ramp[:, None] * ramp[None, :] % window) * (2.0 * np.pi / window)
    cosine = np.cos(angles) / np.sqrt(window)
    sine = np.sin(angles) / np.sqrt(window)
    first = np.block([[cosine, -sine], [sine, cosine]])
    second = np.block([[cosine, sine], [-sine, cosine]])
    tables = []
    for table in (first, second):
        high = table.astype(np.float32).astype(BF16)
        low = (table - high.astype(np.float64)).astype(np.float32).astype(BF16)
        tables.append(np.concatenate([high, low], axis=0))
        tables.append(np.concatenate([high, low], axis=1))
    return tables


def split(value):
    high = value.astype(BF16)
    return high, (value - high.astype(F32)).astype(BF16)


def from_right(value, table):
    high = value.astype(BF16)
    return jnp.dot(jnp.concatenate([high, high], axis=1), table, preferred_element_type=F32)


def from_left(table, value):
    high = value.astype(BF16)
    return jnp.dot(table, jnp.concatenate([high, high], axis=0), preferred_element_type=F32)


STEP_MASKS = (1, 8, 24, 2, 4)


def step_bits(scan):
    return (scan & 1, (scan >> 3 ^ scan >> 4) & 1, scan >> 4 & 1, scan >> 1 & 1, scan >> 2 & 1)


def pair_order(bands):
    even = [scan for scan in range(bands) if scan % 2 == 0]
    return sorted(even, key=step_bits)


def pack_kernel(positions, measured, packed):
    patterns = measured.shape[0]
    slots, rows, window = packed.shape
    packed[...] = jnp.zeros(packed.shape, jnp.int16)
    lane = lax.broadcasted_iota(jnp.int32, (rows - window, window), 1)
    for p in range(patterns):
        row = positions[p, 0]
        column = positions[p, 1]
        tile = column // (3 * window)
        start = column - tile * (3 * window) - 2 * window
        amplitude = jnp.sqrt(measured[p]) * (STEPS / TOP)
        level = jnp.clip(jnp.round(amplitude) - HALF, -HALF, HALF - 1.0)
        packed[tile, 0:window, :] = level.astype(jnp.int32).astype(jnp.int16)
        note = jnp.where(lane == 0, row, jnp.where(lane == 1, start, jnp.where(lane == 2, 1, 0)))
        packed[tile, window:rows, :] = note.astype(jnp.int16)


def main_kernel(
    notes, received, own, margin, probe, first_down, first_across, second_down, second_across,
    probe_sums, keep, give, shifts, strip, total, probe_total, probe_full,
):
    slots = received.shape[0]
    modes = probe.shape[0]
    window = probe.shape[2]
    bands = probe_sums.shape[0]
    height = own.shape[1]
    for part in range(2):
        strip[part, 0] = own[part].astype(BF16).astype(F32)
        strip[part, 1] = margin[part].astype(F32)
        for m in range(modes):
            probe_full[m, part] = probe[m, part].astype(F32)
    total[...] = jnp.zeros(total.shape, F32)
    probe_total[...] = jnp.zeros(probe_total.shape, F32)
    lane = lax.broadcasted_iota(jnp.int32, (window, window), 1)
    row = lax.broadcasted_iota(jnp.int32, (window, window), 0)

    def cut(slot):
        start = jnp.clip(notes[slot, 1], 1, window - 1)
        rows = pl.ds(notes[slot, 0], window)
        both = []
        for part in range(2):
            near = pltpu.roll(strip[part, 0, rows, :], window - start, 1)
            far = pltpu.roll(strip[part, 1, rows, :], window - start, 1)
            both.append(jnp.where(lane < window - start, near, far))
        return both

    def leave(w_re, w_im):
        exits = []
        for m in range(modes):
            p_re, p_im = probe_full[m, 0], probe_full[m, 1]
            exits.append(
                jnp.concatenate([p_re * w_re - p_im * w_im, p_re * w_im + p_im * w_re], axis=1)
            )
        return exits

    def scale_of(slot, blocks):
        power = blocks[0][0] * blocks[0][0]
        for m in range(modes):
            for c in range(2):
                if m or c:
                    power = power + blocks[m][c] * blocks[m][c]
        amplitude = (received[slot, 0:window, :].astype(jnp.int32).astype(F32) + HALF) * (TOP / STEPS)
        return notes[slot, 2].astype(F32) * (1.0 - amplitude * lax.rsqrt(jnp.maximum(power, 0.25)))

    def finish(slot, w_re, w_im, back):
        start = jnp.clip(notes[slot, 1], 1, window - 1)
        rows = pl.ds(notes[slot, 0], window)
        patch_re = jnp.zeros((window, window), F32)
        patch_im = jnp.zeros((window, window), F32)
        for m in range(modes):
            p_re, p_im = probe_full[m, 0], probe_full[m, 1]
            b_re, b_im = back[m]
            patch_re = patch_re + (p_re * b_re + p_im * b_im)
            patch_im = patch_im + (p_re * b_im - p_im * b_re)
            probe_total[2 * m] += w_re * b_re + w_im * b_im
            probe_total[2 * m + 1] += w_re * b_im - w_im * b_re
        for axis, at in ((0, row), (1, lane)):
            change = patch_re * (pltpu.roll(w_re, window - 1, axis) - w_re) + patch_im * (
                pltpu.roll(w_im, window - 1, axis) - w_im
            )
            change = jnp.where(at < window - 1, change, 0.0)
            shifts[slot, pl.ds(axis, 1), :] = jnp.sum(change, axis=0, keepdims=True)
        for part, patch in enumerate((patch_re, patch_im)):
            turned = pltpu.roll(patch.astype(BF16).astype(F32), start, 1)
            total[part, 0, rows, :] += jnp.where(lane >= start, turned, 0.0)
            total[part, 1, rows, :] += jnp.where(lane < start, turned, 0.0)

    def several(slots_now):
        cuts = [cut(slot) for slot in slots_now]
        exits = [e for w in cuts for e in leave(*w)]
        field = both_ways(exits, first_down[...], second_across[...])
        scaled = []
        for u, slot in enumerate(slots_now):
            mine = field[u * modes:(u + 1) * modes]
            scaling = scale_of(slot, mine)
            scaled += [jnp.concatenate([scaling * b[0], scaling * b[1]], axis=1) for b in mine]
        back = both_ways(scaled, second_down[...], first_across[...])
        for u, slot in enumerate(slots_now):
            finish(slot, *cuts[u], back[u * modes:(u + 1) * modes])

    def both_ways(blocks, down, across):
        count = len(blocks)
        half = from_right(jnp.concatenate(blocks, axis=0), down)
        pieces = [
            [half[b * window:(b + 1) * window, c * window:(c + 1) * window] for c in range(2)]
            for b in range(count)
        ]
        stacked = jnp.concatenate(
            [jnp.concatenate([p[c] for p in pieces], axis=1) for c in range(2)], axis=0
        )
        out = from_left(across, stacked)
        return [
            [out[c * window:(c + 1) * window, b * window:(b + 1) * window] for c in range(2)]
            for b in range(count)
        ]

    def step(at, carry):
        several([GROUP * at + u for u in range(GROUP)])
        return carry

    shifts[...] = jnp.zeros(shifts.shape, F32)
    lax.fori_loop(0, slots // GROUP, step, 0)
    mine = lax.axis_index("scan") & 1
    deep = height // bands
    for at, band in enumerate(pair_order(bands)):
        for part in range(2):
            for side in range(2):
                for out, who in ((keep, mine), (give, 1 - mine)):
                    start = pl.multiple_of((band + who) * deep, deep)
                    out[at, part, side] = total[part, side, pl.ds(start, deep), :].astype(out.dtype)
    piece = 2 * modes * window // bands
    for b in range(bands):
        mode, offset = divmod(b * piece, window)
        parts = []
        left = piece
        while left:
            take = min(left, window - offset)
            parts.append(probe_total[mode, offset:offset + take, :])
            mode, offset, left = mode + 1, 0, left - take
        parts.append(jnp.zeros((probe_sums.shape[1] - piece, window), F32))
        probe_sums[b] = jnp.concatenate(parts, axis=0).astype(BF16)


def pack(positions, measured, slots):
    window = measured.shape[2]
    return pl.pallas_call(
        pack_kernel,
        out_shape=jax.ShapeDtypeStruct((slots, window + 16, window), jnp.int16),
        in_specs=[
            pl.BlockSpec(memory_space=pltpu.SMEM),
            pl.BlockSpec(memory_space=pltpu.VMEM),
        ],
        out_specs=pl.BlockSpec(memory_space=pltpu.VMEM),
        compiler_params=pltpu.CompilerParams(vmem_limit_bytes=16 * 2**20),
    )(positions, measured)


def compute(notes, received, object_field, margin, probe, bands):
    modes, window = probe.shape[0], probe.shape[2]
    slots = received.shape[0]
    height = object_field.shape[1]
    tables = [jnp.asarray(table) for table in dft_tables(window)]
    vmem = pl.BlockSpec(memory_space=pltpu.VMEM)

    def whole(shape):
        return pl.BlockSpec(shape, lambda i: (0,) * len(shape))

    rows = -(-(2 * modes * window // bands) // 16) * 16
    half = (bands // 2, 2, 2, height // bands, window)
    return pl.pallas_call(
        main_kernel,
        grid=(1,),
        out_shape=(
            jax.ShapeDtypeStruct((bands, rows, window), BF16),
            jax.ShapeDtypeStruct(half, F32),
            jax.ShapeDtypeStruct(half, BF16),
            jax.ShapeDtypeStruct((slots, 8, window), F32),
        ),
        in_specs=[
            pl.BlockSpec(memory_space=pltpu.SMEM),
            whole(received.shape),
            pl.BlockSpec((2, height, window), lambda i: (0, 0, 2)),
            whole(margin.shape),
            whole(probe.shape),
        ] + [whole(table.shape) for table in tables],
        out_specs=(whole((bands, rows, window)), whole(half), whole(half), whole((slots, 8, window))),
        scratch_shapes=[
            pltpu.VMEM((2, 2, height, window), F32),
            pltpu.VMEM((2, 2, height, window), F32),
            pltpu.VMEM((2 * modes, window, window), F32),
            pltpu.VMEM((modes, 2, window, window), F32),
        ],
        compiler_params=pltpu.CompilerParams(vmem_limit_bytes=40 * 2**20),
    )(notes, received, object_field, margin, probe, *tables)


def exchange(value, axis):
    return lax.all_to_all(value, axis, split_axis=0, concat_axis=0, tiled=True)


def local(object_field, probe, measured, positions):
    tiles = lax.axis_size("tile")
    bands = lax.axis_size("scan")
    width = object_field.shape[2]
    height = object_field.shape[1]
    modes, window = probe.shape[0], probe.shape[2]
    patterns = measured.shape[0]
    deep = height // bands
    piece = 2 * modes * window // bands
    margin = lax.ppermute(
        object_field[:, :, :window].astype(BF16), "tile", [(t, t - 1) for t in range(1, tiles)]
    )
    received = exchange(pack(positions, measured, tiles), "tile")
    notes = received[:, window, :3].astype(jnp.int32)
    probe_sums, keep, give, shifts = compute(notes, received, object_field, margin, probe, bands)
    bits = step_bits(lax.axis_index("scan"))
    for at, mask in enumerate(STEP_MASKS):
        pairs = [(scan, scan ^ mask) for scan in range(bands)]
        current = keep + lax.ppermute(give, "scan", pairs).astype(F32)
        if at + 1 < len(STEP_MASKS):
            half = current.shape[0] // 2
            upper = bits[at + 1] == 1
            keep = jnp.where(upper, current[half:], current[:half])
            give = jnp.where(upper, current[:half], current[half:])
            if at == 0:
                give = give.astype(BF16)
    strips = current[0]
    gathered = jnp.sum(exchange(probe_sums, "scan").astype(F32), axis=0)
    spilled = lax.ppermute(strips[:, 1], "tile", [(t, t + 1) for t in range(tiles - 1)])
    object_grad = jnp.concatenate(
        [spilled, jnp.zeros((2, deep, width - 2 * window), F32), strips[:, 0]], axis=2
    )
    own_piece = gathered[:piece]
    outgoing = jnp.concatenate(
        [jnp.broadcast_to(own_piece[None], (tiles, piece, window)), shifts], axis=1
    )
    mixed = exchange(outgoing, "tile")
    full_piece = jnp.sum(mixed[:, :piece], axis=0) / math.sqrt(patterns * bands * tiles)
    probe_grad = exchange(
        jnp.broadcast_to(full_piece[None], (bands, piece, window)), "scan"
    ).reshape(modes, 2, window, window)
    per_tile = jnp.sum(mixed[:, piece:piece + 2], axis=2) / window
    left_tile = positions[:, 1] // width
    hits = left_tile[:, None] == jnp.arange(tiles, dtype=jnp.int32)[None, :]
    position_grad = jnp.sum(jnp.where(hits[:, :, None], per_tile[None], 0.0), axis=1)
    return (object_grad, probe_grad, position_grad)


def solution(mesh):
    return jax.shard_map(
        local,
        mesh=mesh,
        in_specs=(
            P(None, None, "tile"),
            P(),
            P(("scan", "tile"), None, None),
            P(("scan", "tile"), None),
        ),
        out_specs=(P(None, "scan", "tile"), P(), P(("scan", "tile"), None)),
        check_vma=False,
    )
```

```python
import math

import jax
import jax.numpy as jnp
import numpy as np
from jax import lax
from jax.experimental import pallas as pl
from jax.experimental.pallas import tpu as pltpu
from jax.sharding import PartitionSpec as P

F32 = jnp.float32
BF16 = jnp.bfloat16
TOP = math.sqrt(12.0)
STEPS = 65535.0
HALF = 32768.0
GROUP = 4
LAG = 1


def dft_tables(window):
    ramp = np.arange(window)
    angles = (ramp[:, None] * ramp[None, :] % window) * (2.0 * np.pi / window)
    cosine = np.cos(angles) / np.sqrt(window)
    sine = np.sin(angles) / np.sqrt(window)
    first = np.block([[cosine, -sine], [sine, cosine]])
    second = np.block([[cosine, sine], [-sine, cosine]])
    down, across = [], []
    for table in (first, second):
        high = table.astype(np.float32).astype(BF16)
        low = (table - high.astype(np.float64)).astype(np.float32).astype(BF16)
        down.append(np.concatenate([high, low], axis=0))
        across.append(np.concatenate([high, low], axis=1))
    return np.stack(down), np.stack(across)


def split(value):
    high = value.astype(BF16)
    return high, (value - high.astype(F32)).astype(BF16)


def from_right(value, table):
    high = value.astype(BF16)
    return jnp.dot(jnp.concatenate([high, high], axis=1), table, preferred_element_type=F32)


def from_left(table, value):
    high = value.astype(BF16)
    return jnp.dot(table, jnp.concatenate([high, high], axis=0), preferred_element_type=F32)


def pack_kernel(positions, measured, low, packed):
    del low
    patterns = measured.shape[0]
    slots, rows, window = packed.shape
    packed[...] = jnp.zeros(packed.shape, jnp.int16)
    lane = lax.broadcasted_iota(jnp.int32, (rows - window, window), 1)
    for p in range(patterns):
        row = positions[0, p]
        column = positions[1, p]
        tile = column // (3 * window)
        start = column - tile * (3 * window) - 2 * window
        amplitude = jnp.sqrt(measured[p]) * (STEPS / TOP)
        level = jnp.clip(jnp.round(amplitude) - HALF, -HALF, HALF - 1.0)
        packed[tile, 0:window, :] = level.astype(jnp.int32).astype(jnp.int16)
        note = jnp.where(lane == 0, row, jnp.where(lane == 1, start, jnp.where(lane == 2, 1, 0)))
        packed[tile, window:rows, :] = note.astype(jnp.int16)


def main_kernel(
    notes, received, own, margin, probe, down, across,
    sums, shifts, strip, total, probe_total, probe_full,
):
    slots = received.shape[0]
    modes = probe.shape[0]
    window = probe.shape[2]
    bands = sums.shape[0]
    height = own.shape[1]
    for part in range(2):
        strip[part, 0] = own[part].astype(BF16).astype(F32)
        strip[part, 1] = margin[part].astype(F32)
        for m in range(modes):
            probe_full[m, part] = probe[m, part].astype(F32)
    total[...] = jnp.zeros(total.shape, F32)
    probe_total[...] = jnp.zeros(probe_total.shape, F32)
    lane = lax.broadcasted_iota(jnp.int32, (window, window), 1)
    row = lax.broadcasted_iota(jnp.int32, (window, window), 0)

    def cut(slot):
        start = jnp.clip(notes[slot, 1], 1, window - 1)
        rows = pl.ds(notes[slot, 0], window)
        both = []
        for part in range(2):
            near = pltpu.roll(strip[part, 0, rows, :], window - start, 1)
            far = pltpu.roll(strip[part, 1, rows, :], window - start, 1)
            both.append(jnp.where(lane < window - start, near, far))
        return both

    def leave(w_re, w_im):
        exits = []
        for m in range(modes):
            p_re, p_im = probe_full[m, 0], probe_full[m, 1]
            exits.append(
                jnp.concatenate([p_re * w_re - p_im * w_im, p_re * w_im + p_im * w_re], axis=1)
            )
        return exits

    def scale_of(slot, blocks):
        power = blocks[0][0] * blocks[0][0]
        for m in range(modes):
            for c in range(2):
                if m or c:
                    power = power + blocks[m][c] * blocks[m][c]
        amplitude = (received[slot, 0:window, :].astype(jnp.int32).astype(F32) + HALF) * (TOP / STEPS)
        return notes[slot, 2].astype(F32) * (1.0 - amplitude * lax.rsqrt(jnp.maximum(power, 0.25)))

    def finish(slot, w_re, w_im, back):
        start = jnp.clip(notes[slot, 1], 1, window - 1)
        rows = pl.ds(notes[slot, 0], window)
        patch_re = jnp.zeros((window, window), F32)
        patch_im = jnp.zeros((window, window), F32)
        for m in range(modes):
            p_re, p_im = probe_full[m, 0], probe_full[m, 1]
            b_re, b_im = back[m]
            patch_re = patch_re + (p_re * b_re + p_im * b_im)
            patch_im = patch_im + (p_re * b_im - p_im * b_re)
            probe_total[2 * m] += w_re * b_re + w_im * b_im
            probe_total[2 * m + 1] += w_re * b_im - w_im * b_re
        for axis, at in ((0, row), (1, lane)):
            change = patch_re * (pltpu.roll(w_re, window - 1, axis) - w_re) + patch_im * (
                pltpu.roll(w_im, window - 1, axis) - w_im
            )
            change = jnp.where(at < window - 1, change, 0.0)
            shifts[slot, pl.ds(axis, 1), :] = jnp.sum(change, axis=0, keepdims=True)
        for part, patch in enumerate((patch_re, patch_im)):
            turned = pltpu.roll(patch.astype(BF16).astype(F32), start, 1)
            total[part, 0, rows, :] += jnp.where(lane >= start, turned, 0.0)
            total[part, 1, rows, :] += jnp.where(lane < start, turned, 0.0)

    def stages(slots_now):
        cuts = [cut(slot) for slot in slots_now]
        exits = [e for w in cuts for e in leave(*w)]
        half = rows_first(exits, down[0])
        yield
        field = columns_next(half, across[1])
        yield
        scaled = []
        for u, slot in enumerate(slots_now):
            mine = field[u * modes:(u + 1) * modes]
            scaling = scale_of(slot, mine)
            scaled += [jnp.concatenate([scaling * b[0], scaling * b[1]], axis=1) for b in mine]
        half = rows_first(scaled, down[1])
        yield
        back = columns_next(half, across[0])
        yield
        for u, slot in enumerate(slots_now):
            finish(slot, *cuts[u], back[u * modes:(u + 1) * modes])

    def rows_first(blocks, down):
        half = from_right(jnp.concatenate(blocks, axis=0), down)
        return [
            [half[b * window:(b + 1) * window, c * window:(c + 1) * window] for c in range(2)]
            for b in range(len(blocks))
        ]

    def columns_next(pieces, across):
        stacked = jnp.concatenate(
            [jnp.concatenate([p[c] for p in pieces], axis=1) for c in range(2)], axis=0
        )
        out = from_left(across, stacked)
        return [
            [out[c * window:(c + 1) * window, b * window:(b + 1) * window] for c in range(2)]
            for b in range(len(pieces))
        ]

    shifts[...] = jnp.zeros(shifts.shape, F32)
    flows = [stages(range(at, at + GROUP)) for at in range(0, slots, GROUP)]
    for tick in range(5 + LAG * (len(flows) - 1)):
        for at, flow in enumerate(flows):
            if 0 <= tick - LAG * at < 5:
                next(flow, None)
    deep = height // bands
    piece = 2 * modes * window // bands
    for b in range(bands):
        for part in range(2):
            for side in range(2):
                at = (2 * part + side) * deep
                sums[b, at:at + deep, :] = total[part, side, b * deep:(b + 1) * deep, :].astype(BF16)
        mode, offset = divmod(b * piece, window)
        parts = []
        left = piece
        while left:
            take = min(left, window - offset)
            parts.append(probe_total[mode, offset:offset + take, :])
            mode, offset, left = mode + 1, 0, left - take
        parts.append(jnp.zeros((sums.shape[1] - 4 * deep - piece, window), F32))
        sums[b, 4 * deep:, :] = jnp.concatenate(parts, axis=0).astype(BF16)


def pack(positions, measured, low, slots):
    window = measured.shape[2]
    return pl.pallas_call(
        pack_kernel,
        out_shape=jax.ShapeDtypeStruct((slots, window + 16, window), jnp.int16),
        in_specs=[
            pl.BlockSpec(memory_space=pltpu.SMEM),
            pl.BlockSpec(memory_space=pltpu.VMEM),
            pl.BlockSpec(memory_space=pl.ANY),
        ],
        out_specs=pl.BlockSpec(memory_space=pltpu.VMEM),
        compiler_params=pltpu.CompilerParams(vmem_limit_bytes=16 * 2**20),
    )(positions.T, measured, low)


def compute(notes, received, object_field, margin, probe, bands):
    modes, window = probe.shape[0], probe.shape[2]
    slots = received.shape[0]
    height = object_field.shape[1]
    tables = [jnp.asarray(table) for table in dft_tables(window)]
    vmem = pl.BlockSpec(memory_space=pltpu.VMEM)

    def whole(shape):
        return pl.BlockSpec(shape, lambda i: (0,) * len(shape))

    rows = 4 * (height // bands) + -(-(2 * modes * window // bands) // 16) * 16
    return pl.pallas_call(
        main_kernel,
        grid=(1,),
        out_shape=(
            jax.ShapeDtypeStruct((bands, rows, window), BF16),
            jax.ShapeDtypeStruct((slots, 8, window), F32),
        ),
        in_specs=[
            pl.BlockSpec(memory_space=pltpu.SMEM),
            whole(received.shape),
            pl.BlockSpec((2, height, window), lambda i: (0, 0, 2)),
            whole(margin.shape),
            whole(probe.shape),
        ] + [whole(table.shape) for table in tables],
        out_specs=(whole((bands, rows, window)), whole((slots, 8, window))),
        scratch_shapes=[
            pltpu.VMEM((2, 2, height, window), F32),
            pltpu.VMEM((2, 2, height, window), F32),
            pltpu.VMEM((2 * modes, window, window), F32),
            pltpu.VMEM((modes, 2, window, window), F32),
        ],
        compiler_params=pltpu.CompilerParams(vmem_limit_bytes=40 * 2**20),
    )(notes, received, object_field, margin, probe, *tables)


def exchange(value, axis):
    return lax.all_to_all(value, axis, split_axis=0, concat_axis=0, tiled=True)


def local(object_field, probe, measured, positions):
    tiles = lax.axis_size("tile")
    bands = lax.axis_size("scan")
    width = object_field.shape[2]
    height = object_field.shape[1]
    modes, window = probe.shape[0], probe.shape[2]
    patterns = measured.shape[0]
    deep = height // bands
    piece = 2 * modes * window // bands
    low = object_field[:, :, :window].astype(BF16)
    margin = lax.ppermute(low, "tile", [(t, t - 1) for t in range(1, tiles)])
    received = exchange(pack(positions, measured, low, tiles), "tile")
    notes = received[:, window, :3].astype(jnp.int32)
    sums, shifts = compute(notes, received, object_field, margin, probe, bands)
    gathered = jnp.sum(exchange(sums, "scan").astype(F32), axis=0)
    strips = gathered[:4 * deep].reshape(2, 2, deep, window)
    own_piece = gathered[4 * deep:4 * deep + piece]
    outgoing = jnp.concatenate(
        [jnp.broadcast_to(own_piece[None], (tiles, piece, window)), shifts], axis=1
    )
    mixed = exchange(outgoing, "tile")
    full_piece = jnp.sum(mixed[:, :piece], axis=0) / math.sqrt(patterns * bands * tiles)
    copies = jnp.broadcast_to(full_piece.astype(BF16)[None], (bands, piece, window))
    probe_grad = exchange(copies, "scan").astype(F32).reshape(modes, 2, window, window)
    per_tile = jnp.sum(mixed[:, piece:piece + 2], axis=2) / window
    left_tile = positions[:, 1] // width
    hits = left_tile[:, None] == jnp.arange(tiles, dtype=jnp.int32)[None, :]
    position_grad = jnp.sum(jnp.where(hits[:, :, None], per_tile[None], 0.0), axis=1)
    spilled = lax.ppermute(strips[:, 1], "tile", [(t, t + 1) for t in range(tiles - 1)])
    object_grad = jnp.concatenate(
        [spilled, jnp.zeros((2, deep, width - 2 * window), F32), strips[:, 0]], axis=2
    )
    return (object_grad, probe_grad, position_grad)


def solution(mesh):
    return jax.shard_map(
        local,
        mesh=mesh,
        in_specs=(
            P(None, None, "tile"),
            P(),
            P(("scan", "tile"), None, None),
            P(("scan", "tile"), None),
        ),
        out_specs=(P(None, "scan", "tile"), P(), P(("scan", "tile"), None)),
        check_vma=False,
    )
```

```python
import math

import jax
import jax.numpy as jnp
import numpy as np
from jax import lax
from jax.experimental import pallas as pl
from jax.experimental.pallas import tpu as pltpu
from jax.sharding import PartitionSpec as P

F32 = jnp.float32
BF16 = jnp.bfloat16
TOP = math.sqrt(12.0)
STEPS = 65535.0
HALF = 32768.0
GROUP = 4
LAG = 1


def dft_tables(window):
    ramp = np.arange(window)
    angles = (ramp[:, None] * ramp[None, :] % window) * (2.0 * np.pi / window)
    cosine = np.cos(angles) / np.sqrt(window)
    sine = np.sin(angles) / np.sqrt(window)
    first = np.block([[cosine, -sine], [sine, cosine]])
    second = np.block([[cosine, sine], [-sine, cosine]])
    down, across = [], []
    for table in (first, second):
        high = table.astype(np.float32).astype(BF16)
        low = (table - high.astype(np.float64)).astype(np.float32).astype(BF16)
        down.append(np.concatenate([high, low], axis=0))
        across.append(np.concatenate([high, low], axis=1))
    return np.stack(down), np.stack(across)


def split(value):
    high = value.astype(BF16)
    return high, (value - high.astype(F32)).astype(BF16)


def from_right(value, table):
    high = value.astype(BF16)
    return jnp.dot(jnp.concatenate([high, high], axis=1), table, preferred_element_type=F32)


def from_left(table, value):
    high = value.astype(BF16)
    return jnp.dot(table, jnp.concatenate([high, high], axis=0), preferred_element_type=F32)


def pack_kernel(positions, measured, packed, places, loaded, place_sem, load_sems):
    patterns = measured.shape[0]
    slots, rows, window = packed.shape
    place = pltpu.make_async_copy(positions, places, place_sem)
    place.start()
    loads = [
        pltpu.make_async_copy(measured.at[p], loaded.at[p], load_sems.at[p]) for p in range(patterns)
    ]
    for load in loads:
        load.start()
    packed[...] = jnp.zeros(packed.shape, jnp.int16)
    lane = lax.broadcasted_iota(jnp.int32, (rows - window, window), 1)
    place.wait()
    for p in range(patterns):
        row = places[0, p]
        column = places[1, p]
        tile = column // (3 * window)
        start = column - tile * (3 * window) - 2 * window
        note = jnp.where(lane == 0, row, jnp.where(lane == 1, start, jnp.where(lane == 2, 1, 0)))
        packed[tile, window:rows, :] = note.astype(jnp.int16)
        loads[p].wait()
        amplitude = jnp.sqrt(loaded[p]) * (STEPS / TOP)
        level = jnp.clip(jnp.round(amplitude) - HALF, -HALF, HALF - 1.0)
        packed[tile, 0:window, :] = level.astype(jnp.int32).astype(jnp.int16)


def main_kernel(
    notes, received, own, margin, probe, down, across,
    probe_sums, sums, shifts, strip, total, probe_total, probe_full,
    probe_near, probe_sem,
):
    slots = received.shape[0]
    modes = probe.shape[0]
    window = probe.shape[2]
    bands = sums.shape[0]
    height = own.shape[1]
    fetch = pltpu.make_async_copy(probe, probe_near, probe_sem)
    fetch.start()
    for part in range(2):
        strip[part, 0] = own[part].astype(BF16).astype(F32)
        strip[part, 1] = margin[part].astype(F32)
    total[...] = jnp.zeros(total.shape, F32)
    probe_total[...] = jnp.zeros(probe_total.shape, F32)
    fetch.wait()
    probe_full[...] = probe_near[...].astype(F32)
    lane = lax.broadcasted_iota(jnp.int32, (window, window), 1)
    row = lax.broadcasted_iota(jnp.int32, (window, window), 0)

    def cut(slot):
        start = jnp.clip(notes[slot, 1], 1, window - 1)
        rows = pl.ds(notes[slot, 0], window)
        both = []
        for part in range(2):
            near = pltpu.roll(strip[part, 0, rows, :], window - start, 1)
            far = pltpu.roll(strip[part, 1, rows, :], window - start, 1)
            both.append(jnp.where(lane < window - start, near, far))
        return both

    def leave(w_re, w_im):
        exits = []
        for m in range(modes):
            p_re, p_im = probe_full[m, 0], probe_full[m, 1]
            exits.append(
                jnp.concatenate([p_re * w_re - p_im * w_im, p_re * w_im + p_im * w_re], axis=1)
            )
        return exits

    def scale_of(slot, blocks):
        power = blocks[0][0] * blocks[0][0]
        for m in range(modes):
            for c in range(2):
                if m or c:
                    power = power + blocks[m][c] * blocks[m][c]
        amplitude = (received[slot, 0:window, :].astype(jnp.int32).astype(F32) + HALF) * (TOP / STEPS)
        return notes[slot, 2].astype(F32) * (1.0 - amplitude * lax.rsqrt(jnp.maximum(power, 0.25)))

    def finish(slot, w_re, w_im, back):
        start = jnp.clip(notes[slot, 1], 1, window - 1)
        rows = pl.ds(notes[slot, 0], window)
        patch_re = jnp.zeros((window, window), F32)
        patch_im = jnp.zeros((window, window), F32)
        for m in range(modes):
            p_re, p_im = probe_full[m, 0], probe_full[m, 1]
            b_re, b_im = back[m]
            patch_re = patch_re + (p_re * b_re + p_im * b_im)
            patch_im = patch_im + (p_re * b_im - p_im * b_re)
            probe_total[2 * m] += w_re * b_re + w_im * b_im
            probe_total[2 * m + 1] += w_re * b_im - w_im * b_re
        for axis, at in ((0, row), (1, lane)):
            change = patch_re * (pltpu.roll(w_re, window - 1, axis) - w_re) + patch_im * (
                pltpu.roll(w_im, window - 1, axis) - w_im
            )
            change = jnp.where(at < window - 1, change, 0.0)
            shifts[slot, pl.ds(axis, 1), :] = jnp.sum(change, axis=0, keepdims=True)
        for part, patch in enumerate((patch_re, patch_im)):
            turned = pltpu.roll(patch.astype(BF16).astype(F32), start, 1)
            total[part, 0, rows, :] += jnp.where(lane >= start, turned, 0.0)
            total[part, 1, rows, :] += jnp.where(lane < start, turned, 0.0)

    def stages(slots_now):
        cuts = [cut(slot) for slot in slots_now]
        exits = [e for w in cuts for e in leave(*w)]
        half = rows_first(exits, down[0])
        yield
        field = columns_next(half, across[1])
        yield
        scaled = []
        for u, slot in enumerate(slots_now):
            mine = field[u * modes:(u + 1) * modes]
            scaling = scale_of(slot, mine)
            scaled += [jnp.concatenate([scaling * b[0], scaling * b[1]], axis=1) for b in mine]
        half = rows_first(scaled, down[1])
        yield
        back = columns_next(half, across[0])
        yield
        for u, slot in enumerate(slots_now):
            finish(slot, *cuts[u], back[u * modes:(u + 1) * modes])

    def rows_first(blocks, down):
        half = from_right(jnp.concatenate(blocks, axis=0), down)
        return [
            [half[b * window:(b + 1) * window, c * window:(c + 1) * window] for c in range(2)]
            for b in range(len(blocks))
        ]

    def columns_next(pieces, across):
        stacked = jnp.concatenate(
            [jnp.concatenate([p[c] for p in pieces], axis=1) for c in range(2)], axis=0
        )
        out = from_left(across, stacked)
        return [
            [out[c * window:(c + 1) * window, b * window:(b + 1) * window] for c in range(2)]
            for b in range(len(pieces))
        ]

    shifts[...] = jnp.zeros(shifts.shape, F32)
    flows = [stages(range(at, at + GROUP)) for at in range(0, slots, GROUP)]
    for tick in range(5 + LAG * (len(flows) - 1)):
        for at, flow in enumerate(flows):
            if 0 <= tick - LAG * at < 5:
                next(flow, None)
    for b in range(bands):
        deep = height // bands
        for part in range(2):
            for side in range(2):
                at = (2 * part + side) * deep
                sums[b, at:at + deep, :] = total[part, side, b * deep:(b + 1) * deep, :].astype(BF16)
    piece = 2 * modes * window // slots
    for t in range(slots):
        mode, offset = divmod(t * piece, window)
        left, at = piece, 0
        while left:
            take = min(left, window - offset)
            probe_sums[t, at:at + take, :] = probe_total[mode, offset:offset + take, :].astype(BF16)
            mode, offset, left, at = mode + 1, 0, left - take, at + take
        probe_sums[t, piece:, :] = jnp.concatenate(split(shifts[t]), axis=0)


def pack(positions, measured, slots):
    patterns, window = measured.shape[0], measured.shape[2]
    return pl.pallas_call(
        pack_kernel,
        out_shape=jax.ShapeDtypeStruct((slots, window + 16, window), jnp.int16),
        in_specs=[pl.BlockSpec(memory_space=pltpu.HBM)] * 2,
        out_specs=pl.BlockSpec(memory_space=pltpu.VMEM),
        scratch_shapes=[
            pltpu.SMEM((2, patterns), jnp.int32),
            pltpu.VMEM(measured.shape, F32),
            pltpu.SemaphoreType.DMA,
            pltpu.SemaphoreType.DMA((patterns,)),
        ],
        compiler_params=pltpu.CompilerParams(vmem_limit_bytes=60 * 2**20),
    )(positions.T, measured)


def compute(notes, received, object_field, margin, probe, bands):
    modes, window = probe.shape[0], probe.shape[2]
    slots = received.shape[0]
    height = object_field.shape[1]
    tables = [jnp.asarray(table) for table in dft_tables(window)]
    vmem = pl.BlockSpec(memory_space=pltpu.VMEM)

    def whole(shape):
        return pl.BlockSpec(shape, lambda i: (0,) * len(shape))

    probe_shape = (slots, 2 * modes * window // slots + 16, window)
    sums_shape = (bands, 4 * (height // bands), window)
    return pl.pallas_call(
        main_kernel,
        grid=(1,),
        out_shape=(
            jax.ShapeDtypeStruct(probe_shape, BF16),
            jax.ShapeDtypeStruct(sums_shape, BF16),
        ),
        in_specs=[
            pl.BlockSpec(memory_space=pltpu.SMEM),
            whole(received.shape),
            pl.BlockSpec((2, height, window), lambda i: (0, 0, 2)),
            whole(margin.shape),
            pl.BlockSpec(memory_space=pltpu.HBM),
        ] + [whole(table.shape) for table in tables],
        out_specs=(whole(probe_shape), whole(sums_shape)),
        scratch_shapes=[
            pltpu.VMEM((slots, 8, window), F32),
            pltpu.VMEM((2, 2, height, window), F32),
            pltpu.VMEM((2, 2, height, window), F32),
            pltpu.VMEM((2 * modes, window, window), F32),
            pltpu.VMEM((modes, 2, window, window), F32),
            pltpu.VMEM((modes, 2, window, window), BF16),
            pltpu.SemaphoreType.DMA,
        ],
        compiler_params=pltpu.CompilerParams(vmem_limit_bytes=40 * 2**20),
    )(notes, received, object_field, margin, probe, *tables)


def exchange(value, axis):
    return lax.all_to_all(value, axis, split_axis=0, concat_axis=0, tiled=True)


def local(object_field, probe, measured, positions):
    tiles = lax.axis_size("tile")
    bands = lax.axis_size("scan")
    width = object_field.shape[2]
    height = object_field.shape[1]
    modes, window = probe.shape[0], probe.shape[2]
    patterns = measured.shape[0]
    deep = height // bands
    piece = 2 * modes * window // tiles
    margin = lax.ppermute(
        object_field[:, :, :window].astype(BF16), "tile", [(t, t - 1) for t in range(1, tiles)]
    )
    received = exchange(pack(positions, measured, tiles), "tile")
    notes = received[:, window, :3].astype(jnp.int32)
    probe_sums, sums = compute(notes, received, object_field, margin, probe, bands)
    mixed = exchange(probe_sums, "tile").astype(F32)
    tile_piece = jnp.sum(mixed[:, :piece], axis=0).astype(BF16)
    everything = exchange(
        jnp.concatenate([sums, jnp.broadcast_to(tile_piece[None], (bands, piece, window))], axis=1),
        "scan",
    )
    gathered = jnp.sum(everything.astype(F32), axis=0)
    full_piece = gathered[4 * deep:] / math.sqrt(patterns * bands * tiles)
    probe_grad = exchange(
        jnp.broadcast_to(full_piece.astype(BF16)[None], (tiles, piece, window)), "tile"
    ).astype(F32).reshape(modes, 2, window, window)
    strips = gathered[:4 * deep].reshape(2, 2, deep, window)
    spilled = lax.ppermute(strips[:, 1], "tile", [(t, t + 1) for t in range(tiles - 1)])
    object_grad = jnp.concatenate(
        [spilled, jnp.zeros((2, deep, width - 2 * window), F32), strips[:, 0]], axis=2
    )
    per_tile = jnp.sum(mixed[:, piece:piece + 2] + mixed[:, piece + 8:piece + 10], axis=2) / window
    left_tile = positions[:, 1] // width
    hits = left_tile[:, None] == jnp.arange(tiles, dtype=jnp.int32)[None, :]
    position_grad = jnp.sum(jnp.where(hits[:, :, None], per_tile[None], 0.0), axis=1)
    return (object_grad, probe_grad, position_grad)


def solution(mesh):
    return jax.shard_map(
        local,
        mesh=mesh,
        in_specs=(
            P(None, None, "tile"),
            P(),
            P(("scan", "tile"), None, None),
            P(("scan", "tile"), None),
        ),
        out_specs=(P(None, "scan", "tile"), P(), P(("scan", "tile"), None)),
        check_vma=False,
    )
```

```python
import math

import jax
import jax.numpy as jnp
import numpy as np
from jax import lax
from jax.experimental import pallas as pl
from jax.experimental.pallas import tpu as pltpu
from jax.sharding import PartitionSpec as P

F32 = jnp.float32
BF16 = jnp.bfloat16
TOP = math.sqrt(12.0)
STEPS = 65535.0
HALF = 32768.0
GROUP = 4
LAG = 1


def dft_tables(window):
    ramp = np.arange(window)
    angles = (ramp[:, None] * ramp[None, :] % window) * (2.0 * np.pi / window)
    cosine = np.cos(angles) / np.sqrt(window)
    sine = np.sin(angles) / np.sqrt(window)
    first = np.block([[cosine, -sine], [sine, cosine]])
    second = np.block([[cosine, sine], [-sine, cosine]])
    tables = []
    for table in (first, second):
        high = table.astype(np.float32).astype(BF16)
        low = (table - high.astype(np.float64)).astype(np.float32).astype(BF16)
        tables += [high, low]
    return [np.stack(tables)]


def split(value):
    high = value.astype(BF16)
    return high, (value - high.astype(F32)).astype(BF16)


def from_right(value, table):
    high = value.astype(BF16)
    return jnp.dot(jnp.concatenate([high, high], axis=1), table, preferred_element_type=F32)


def from_left(table, value):
    high = value.astype(BF16)
    return jnp.dot(table, jnp.concatenate([high, high], axis=0), preferred_element_type=F32)


def pack_kernel(positions, measured, packed, places, loaded, place_sem, load_sems):
    patterns = measured.shape[0]
    slots, rows, window = packed.shape
    place = pltpu.make_async_copy(positions, places, place_sem)
    place.start()
    loads = [
        pltpu.make_async_copy(measured.at[p], loaded.at[p], load_sems.at[p]) for p in range(patterns)
    ]
    for load in loads:
        load.start()
    packed[...] = jnp.zeros(packed.shape, jnp.int16)
    lane = lax.broadcasted_iota(jnp.int32, (rows - window, window), 1)
    place.wait()
    for p in range(patterns):
        row = places[0, p]
        column = places[1, p]
        tile = column // (3 * window)
        start = column - tile * (3 * window) - 2 * window
        note = jnp.where(lane == 0, row, jnp.where(lane == 1, start, jnp.where(lane == 2, 1, 0)))
        packed[tile, window:rows, :] = note.astype(jnp.int16)
        loads[p].wait()
        amplitude = jnp.sqrt(loaded[p]) * (STEPS / TOP)
        level = jnp.clip(jnp.round(amplitude) - HALF, -HALF, HALF - 1.0)
        packed[tile, 0:window, :] = level.astype(jnp.int32).astype(jnp.int16)


def main_kernel(
    notes, received, own, margin, probe, tables,
    probe_sums, sums, shifts, strip, total, probe_total, probe_full,
    probe_near, probe_sem,
):
    slots = received.shape[0]
    modes = probe.shape[0]
    window = probe.shape[2]
    bands = sums.shape[0]
    height = own.shape[1]
    fetch = pltpu.make_async_copy(probe, probe_near, probe_sem)
    fetch.start()
    for part in range(2):
        strip[part, 0] = own[part].astype(BF16).astype(F32)
        strip[part, 1] = margin[part].astype(F32)
    total[...] = jnp.zeros(total.shape, F32)
    probe_total[...] = jnp.zeros(probe_total.shape, F32)
    fetch.wait()
    probe_full[...] = probe_near[...].astype(F32)
    lane = lax.broadcasted_iota(jnp.int32, (window, window), 1)
    row = lax.broadcasted_iota(jnp.int32, (window, window), 0)

    def cut(slot):
        start = jnp.clip(notes[slot, 1], 1, window - 1)
        rows = pl.ds(notes[slot, 0], window)
        both = []
        for part in range(2):
            near = pltpu.roll(strip[part, 0, rows, :], window - start, 1)
            far = pltpu.roll(strip[part, 1, rows, :], window - start, 1)
            both.append(jnp.where(lane < window - start, near, far))
        return both

    def leave(w_re, w_im):
        exits = []
        for m in range(modes):
            p_re, p_im = probe_full[m, 0], probe_full[m, 1]
            exits.append(
                jnp.concatenate([p_re * w_re - p_im * w_im, p_re * w_im + p_im * w_re], axis=1)
            )
        return exits

    def scale_of(slot, blocks):
        power = blocks[0][0] * blocks[0][0]
        for m in range(modes):
            for c in range(2):
                if m or c:
                    power = power + blocks[m][c] * blocks[m][c]
        amplitude = (received[slot, 0:window, :].astype(jnp.int32).astype(F32) + HALF) * (TOP / STEPS)
        return notes[slot, 2].astype(F32) * (1.0 - amplitude * lax.rsqrt(jnp.maximum(power, 0.25)))

    def finish(slot, w_re, w_im, back):
        start = jnp.clip(notes[slot, 1], 1, window - 1)
        rows = pl.ds(notes[slot, 0], window)
        patch_re = jnp.zeros((window, window), F32)
        patch_im = jnp.zeros((window, window), F32)
        for m in range(modes):
            p_re, p_im = probe_full[m, 0], probe_full[m, 1]
            b_re, b_im = back[m]
            patch_re = patch_re + (p_re * b_re + p_im * b_im)
            patch_im = patch_im + (p_re * b_im - p_im * b_re)
            probe_total[2 * m] += w_re * b_re + w_im * b_im
            probe_total[2 * m + 1] += w_re * b_im - w_im * b_re
        for axis, at in ((0, row), (1, lane)):
            change = patch_re * (pltpu.roll(w_re, window - 1, axis) - w_re) + patch_im * (
                pltpu.roll(w_im, window - 1, axis) - w_im
            )
            change = jnp.where(at < window - 1, change, 0.0)
            shifts[slot, pl.ds(axis, 1), :] = jnp.sum(change, axis=0, keepdims=True)
        for part, patch in enumerate((patch_re, patch_im)):
            turned = pltpu.roll(patch.astype(BF16).astype(F32), start, 1)
            total[part, 0, rows, :] += jnp.where(lane >= start, turned, 0.0)
            total[part, 1, rows, :] += jnp.where(lane < start, turned, 0.0)

    def joined(at, axis):
        return jnp.concatenate([tables[2 * at], tables[2 * at + 1]], axis=axis)

    def stages(slots_now):
        cuts = [cut(slot) for slot in slots_now]
        exits = [e for w in cuts for e in leave(*w)]
        half = rows_first(exits, joined(0, 0))
        yield
        field = columns_next(half, joined(1, 1))
        yield
        scaled = []
        for u, slot in enumerate(slots_now):
            mine = field[u * modes:(u + 1) * modes]
            scaling = scale_of(slot, mine)
            scaled += [jnp.concatenate([scaling * b[0], scaling * b[1]], axis=1) for b in mine]
        half = rows_first(scaled, joined(1, 0))
        yield
        back = columns_next(half, joined(0, 1))
        yield
        for u, slot in enumerate(slots_now):
            finish(slot, *cuts[u], back[u * modes:(u + 1) * modes])

    def rows_first(blocks, down):
        half = from_right(jnp.concatenate(blocks, axis=0), down)
        return [
            [half[b * window:(b + 1) * window, c * window:(c + 1) * window] for c in range(2)]
            for b in range(len(blocks))
        ]

    def columns_next(pieces, across):
        stacked = jnp.concatenate(
            [jnp.concatenate([p[c] for p in pieces], axis=1) for c in range(2)], axis=0
        )
        out = from_left(across, stacked)
        return [
            [out[c * window:(c + 1) * window, b * window:(b + 1) * window] for c in range(2)]
            for b in range(len(pieces))
        ]

    shifts[...] = jnp.zeros(shifts.shape, F32)
    flows = [stages(range(at, at + GROUP)) for at in range(0, slots, GROUP)]
    for tick in range(5 + LAG * (len(flows) - 1)):
        for at, flow in enumerate(flows):
            if 0 <= tick - LAG * at < 5:
                next(flow, None)
    for b in range(bands):
        deep = height // bands
        for part in range(2):
            for side in range(2):
                at = (2 * part + side) * deep
                sums[b, at:at + deep, :] = total[part, side, b * deep:(b + 1) * deep, :].astype(BF16)
    piece = 2 * modes * window // slots
    for t in range(slots):
        mode, offset = divmod(t * piece, window)
        left, at = piece, 0
        while left:
            take = min(left, window - offset)
            probe_sums[t, at:at + take, :] = probe_total[mode, offset:offset + take, :].astype(BF16)
            mode, offset, left, at = mode + 1, 0, left - take, at + take
        probe_sums[t, piece:, :] = jnp.concatenate(split(shifts[t]), axis=0)


def pack(positions, measured, slots):
    patterns, window = measured.shape[0], measured.shape[2]
    return pl.pallas_call(
        pack_kernel,
        out_shape=jax.ShapeDtypeStruct((slots, window + 16, window), jnp.int16),
        in_specs=[pl.BlockSpec(memory_space=pltpu.HBM)] * 2,
        out_specs=pl.BlockSpec(memory_space=pltpu.VMEM),
        scratch_shapes=[
            pltpu.SMEM((2, patterns), jnp.int32),
            pltpu.VMEM(measured.shape, F32),
            pltpu.SemaphoreType.DMA,
            pltpu.SemaphoreType.DMA((patterns,)),
        ],
        compiler_params=pltpu.CompilerParams(vmem_limit_bytes=60 * 2**20),
    )(positions.T, measured)


def compute(notes, received, object_field, margin, probe, bands):
    modes, window = probe.shape[0], probe.shape[2]
    slots = received.shape[0]
    height = object_field.shape[1]
    tables = [jnp.asarray(table) for table in dft_tables(window)]
    vmem = pl.BlockSpec(memory_space=pltpu.VMEM)

    def whole(shape):
        return pl.BlockSpec(shape, lambda i: (0,) * len(shape))

    probe_shape = (slots, 2 * modes * window // slots + 16, window)
    sums_shape = (bands, 4 * (height // bands) + 2 * modes * window // slots, window)
    return pl.pallas_call(
        main_kernel,
        grid=(1,),
        out_shape=(
            jax.ShapeDtypeStruct(probe_shape, BF16),
            jax.ShapeDtypeStruct(sums_shape, BF16),
        ),
        in_specs=[
            pl.BlockSpec(memory_space=pltpu.SMEM),
            whole(received.shape),
            pl.BlockSpec((2, height, window), lambda i: (0, 0, 2)),
            whole(margin.shape),
            pl.BlockSpec(memory_space=pltpu.HBM),
        ] + [whole(table.shape) for table in tables],
        out_specs=(whole(probe_shape), whole(sums_shape)),
        scratch_shapes=[
            pltpu.VMEM((slots, 8, window), F32),
            pltpu.VMEM((2, 2, height, window), F32),
            pltpu.VMEM((2, 2, height, window), F32),
            pltpu.VMEM((2 * modes, window, window), F32),
            pltpu.VMEM((modes, 2, window, window), F32),
            pltpu.VMEM((modes, 2, window, window), BF16),
            pltpu.SemaphoreType.DMA,
        ],
        compiler_params=pltpu.CompilerParams(vmem_limit_bytes=40 * 2**20),
    )(notes, received, object_field, margin, probe, *tables)


def exchange(value, axis):
    return lax.all_to_all(value, axis, split_axis=0, concat_axis=0, tiled=True)


def local(object_field, probe, measured, positions):
    tiles = lax.axis_size("tile")
    bands = lax.axis_size("scan")
    width = object_field.shape[2]
    height = object_field.shape[1]
    modes, window = probe.shape[0], probe.shape[2]
    patterns = measured.shape[0]
    deep = height // bands
    piece = 2 * modes * window // tiles
    margin = lax.ppermute(
        object_field[:, :, :window].astype(BF16), "tile", [(t, t - 1) for t in range(1, tiles)]
    )
    received = exchange(pack(positions, measured, tiles), "tile")
    notes = received[:, window, :3].astype(jnp.int32)
    probe_sums, sums = compute(notes, received, object_field, margin, probe, bands)
    mixed = exchange(probe_sums, "tile").astype(F32)
    tile_piece = jnp.sum(mixed[:, :piece], axis=0).astype(BF16)
    copies = jnp.broadcast_to(tile_piece[None], (bands, piece, window))
    everything = exchange(lax.dynamic_update_slice(sums, copies, (0, 4 * deep, 0)), "scan")
    gathered = jnp.sum(everything.astype(F32), axis=0)
    full_piece = gathered[4 * deep:] / math.sqrt(patterns * bands * tiles)
    probe_grad = exchange(
        jnp.broadcast_to(full_piece.astype(BF16)[None], (tiles, piece, window)), "tile"
    ).astype(F32).reshape(modes, 2, window, window)
    strips = gathered[:4 * deep].reshape(2, 2, deep, window)
    spilled = lax.ppermute(strips[:, 1], "tile", [(t, t + 1) for t in range(tiles - 1)])
    object_grad = jnp.concatenate(
        [spilled, jnp.zeros((2, deep, width - 2 * window), F32), strips[:, 0]], axis=2
    )
    per_tile = jnp.sum(mixed[:, piece:piece + 2] + mixed[:, piece + 8:piece + 10], axis=2) / window
    left_tile = positions[:, 1] // width
    hits = left_tile[:, None] == jnp.arange(tiles, dtype=jnp.int32)[None, :]
    position_grad = jnp.sum(jnp.where(hits[:, :, None], per_tile[None], 0.0), axis=1)
    return (object_grad, probe_grad, position_grad)


def solution(mesh):
    return jax.shard_map(
        local,
        mesh=mesh,
        in_specs=(
            P(None, None, "tile"),
            P(),
            P(("scan", "tile"), None, None),
            P(("scan", "tile"), None),
        ),
        out_specs=(P(None, "scan", "tile"), P(), P(("scan", "tile"), None)),
        check_vma=False,
    )
```

```python
import math

import jax
import jax.numpy as jnp
import numpy as np
from jax import lax
from jax.experimental import pallas as pl
from jax.experimental.pallas import tpu as pltpu
from jax.sharding import PartitionSpec as P

F32 = jnp.float32
BF16 = jnp.bfloat16
TOP = math.sqrt(12.0)
STEPS = 65535.0
HALF = 32768.0
GROUP = 4
LAG = 1


def dft_tables(window):
    ramp = np.arange(window)
    angles = (ramp[:, None] * ramp[None, :] % window) * (2.0 * np.pi / window)
    cosine = np.cos(angles) / np.sqrt(window)
    sine = np.sin(angles) / np.sqrt(window)
    first = np.block([[cosine, -sine], [sine, cosine]])
    second = np.block([[cosine, sine], [-sine, cosine]])
    tables = []
    for table in (first, second):
        high = table.astype(np.float32).astype(BF16)
        low = (table - high.astype(np.float64)).astype(np.float32).astype(BF16)
        tables += [high, low]
    return [np.stack(tables)]


def split(value):
    high = value.astype(BF16)
    return high, (value - high.astype(F32)).astype(BF16)


def from_right(value, table):
    high = value.astype(BF16)
    return jnp.dot(jnp.concatenate([high, high], axis=1), table, preferred_element_type=F32)


def from_left(table, value):
    high = value.astype(BF16)
    return jnp.dot(table, jnp.concatenate([high, high], axis=0), preferred_element_type=F32)


def pack_kernel(positions, measured, packed, places, loaded, place_sem, load_sems):
    patterns = measured.shape[0]
    slots, rows, window = packed.shape
    place = pltpu.make_async_copy(positions, places, place_sem)
    place.start()
    loads = [
        pltpu.make_async_copy(measured.at[p], loaded.at[p], load_sems.at[p]) for p in range(patterns)
    ]
    for load in loads:
        load.start()
    packed[...] = jnp.zeros(packed.shape, jnp.int16)
    lane = lax.broadcasted_iota(jnp.int32, (rows - window, window), 1)
    place.wait()
    for p in range(patterns):
        row = places[0, p]
        column = places[1, p]
        tile = column // (3 * window)
        start = column - tile * (3 * window) - 2 * window
        note = jnp.where(lane == 0, row, jnp.where(lane == 1, start, jnp.where(lane == 2, 1, 0)))
        packed[tile, window:rows, :] = note.astype(jnp.int16)
        loads[p].wait()
        amplitude = jnp.sqrt(loaded[p]) * (STEPS / TOP)
        level = jnp.clip(jnp.round(amplitude) - HALF, -HALF, HALF - 1.0)
        packed[tile, 0:window, :] = level.astype(jnp.int32).astype(jnp.int16)


def main_kernel(
    notes, received, own, margin, probe, tables,
    probe_sums, sums, shifts, strip, total, probe_total, probe_full,
    probe_near, probe_sem,
):
    slots = received.shape[0]
    modes = probe.shape[0]
    window = probe.shape[2]
    bands = sums.shape[0]
    height = own.shape[1]
    fetch = pltpu.make_async_copy(probe, probe_near, probe_sem)
    fetch.start()
    for part in range(2):
        strip[part, 0] = own[part].astype(BF16).astype(F32)
        strip[part, 1] = margin[part].astype(F32)
    total[...] = jnp.zeros(total.shape, F32)
    probe_total[...] = jnp.zeros(probe_total.shape, F32)
    fetch.wait()
    probe_full[...] = probe_near[...].astype(F32)
    lane = lax.broadcasted_iota(jnp.int32, (window, window), 1)
    row = lax.broadcasted_iota(jnp.int32, (window, window), 0)

    def cut(slot):
        start = jnp.clip(notes[slot, 1], 1, window - 1)
        rows = pl.ds(notes[slot, 0], window)
        both = []
        for part in range(2):
            near = pltpu.roll(strip[part, 0, rows, :], window - start, 1)
            far = pltpu.roll(strip[part, 1, rows, :], window - start, 1)
            both.append(jnp.where(lane < window - start, near, far))
        return both

    def leave(w_re, w_im):
        exits = []
        for m in range(modes):
            p_re, p_im = probe_full[m, 0], probe_full[m, 1]
            exits.append(
                jnp.concatenate([p_re * w_re - p_im * w_im, p_re * w_im + p_im * w_re], axis=1)
            )
        return exits

    def scale_of(slot, blocks):
        power = blocks[0][0] * blocks[0][0]
        for m in range(modes):
            for c in range(2):
                if m or c:
                    power = power + blocks[m][c] * blocks[m][c]
        amplitude = (received[slot, 0:window, :].astype(jnp.int32).astype(F32) + HALF) * (TOP / STEPS)
        return notes[slot, 2].astype(F32) * (1.0 - amplitude * lax.rsqrt(jnp.maximum(power, 0.25)))

    def finish(slot, w_re, w_im, back):
        start = jnp.clip(notes[slot, 1], 1, window - 1)
        rows = pl.ds(notes[slot, 0], window)
        patch_re = jnp.zeros((window, window), F32)
        patch_im = jnp.zeros((window, window), F32)
        for m in range(modes):
            p_re, p_im = probe_full[m, 0], probe_full[m, 1]
            b_re, b_im = back[m]
            patch_re = patch_re + (p_re * b_re + p_im * b_im)
            patch_im = patch_im + (p_re * b_im - p_im * b_re)
            probe_total[2 * m] += w_re * b_re + w_im * b_im
            probe_total[2 * m + 1] += w_re * b_im - w_im * b_re
        for axis, at in ((0, row), (1, lane)):
            change = patch_re * (pltpu.roll(w_re, window - 1, axis) - w_re) + patch_im * (
                pltpu.roll(w_im, window - 1, axis) - w_im
            )
            change = jnp.where(at < window - 1, change, 0.0)
            shifts[slot, pl.ds(axis, 1), :] = jnp.sum(change, axis=0, keepdims=True)
        for part, patch in enumerate((patch_re, patch_im)):
            turned = pltpu.roll(patch.astype(BF16).astype(F32), start, 1)
            total[part, 0, rows, :] += jnp.where(lane >= start, turned, 0.0)
            total[part, 1, rows, :] += jnp.where(lane < start, turned, 0.0)

    def joined(at, axis):
        return jnp.concatenate([tables[2 * at], tables[2 * at + 1]], axis=axis)

    def stages(slots_now):
        cuts = [cut(slot) for slot in slots_now]
        exits = [e for w in cuts for e in leave(*w)]
        half = rows_first(exits, joined(0, 0))
        yield
        field = columns_next(half, joined(1, 1))
        yield
        scaled = []
        for u, slot in enumerate(slots_now):
            mine = field[u * modes:(u + 1) * modes]
            scaling = scale_of(slot, mine)
            scaled += [jnp.concatenate([scaling * b[0], scaling * b[1]], axis=1) for b in mine]
        half = rows_first(scaled, joined(1, 0))
        yield
        back = columns_next(half, joined(0, 1))
        yield
        for u, slot in enumerate(slots_now):
            finish(slot, *cuts[u], back[u * modes:(u + 1) * modes])

    def rows_first(blocks, down):
        half = from_right(jnp.concatenate(blocks, axis=0), down)
        return [
            [half[b * window:(b + 1) * window, c * window:(c + 1) * window] for c in range(2)]
            for b in range(len(blocks))
        ]

    def columns_next(pieces, across):
        stacked = jnp.concatenate(
            [jnp.concatenate([p[c] for p in pieces], axis=1) for c in range(2)], axis=0
        )
        out = from_left(across, stacked)
        return [
            [out[c * window:(c + 1) * window, b * window:(b + 1) * window] for c in range(2)]
            for b in range(len(pieces))
        ]

    shifts[...] = jnp.zeros(shifts.shape, F32)
    flows = [stages(range(at, at + GROUP)) for at in range(0, slots, GROUP)]
    for tick in range(5 + LAG * (len(flows) - 1)):
        for at, flow in enumerate(flows):
            if 0 <= tick - LAG * at < 5:
                next(flow, None)
    for b in range(bands):
        deep = height // bands
        for part in range(2):
            for side in range(2):
                at = (2 * part + side) * deep
                sums[b, at:at + deep, :] = total[part, side, b * deep:(b + 1) * deep, :].astype(BF16)
    piece = 2 * modes * window // slots
    for t in range(slots):
        mode, offset = divmod(t * piece, window)
        left, at = piece, 0
        while left:
            take = min(left, window - offset)
            probe_sums[t, at:at + take, :] = probe_total[mode, offset:offset + take, :].astype(BF16)
            mode, offset, left, at = mode + 1, 0, left - take, at + take
        probe_sums[t, piece:, :] = jnp.concatenate(split(shifts[t]), axis=0)


def pack(positions, measured, slots):
    patterns, window = measured.shape[0], measured.shape[2]
    return pl.pallas_call(
        pack_kernel,
        out_shape=jax.ShapeDtypeStruct((slots, window + 16, window), jnp.int16),
        in_specs=[pl.BlockSpec(memory_space=pltpu.HBM)] * 2,
        out_specs=pl.BlockSpec(memory_space=pltpu.VMEM),
        scratch_shapes=[
            pltpu.SMEM((2, patterns), jnp.int32),
            pltpu.VMEM(measured.shape, F32),
            pltpu.SemaphoreType.DMA,
            pltpu.SemaphoreType.DMA((patterns,)),
        ],
        compiler_params=pltpu.CompilerParams(vmem_limit_bytes=60 * 2**20),
    )(positions.T, measured)


def compute(notes, received, object_field, margin, probe, bands):
    modes, window = probe.shape[0], probe.shape[2]
    slots = received.shape[0]
    height = object_field.shape[1]
    tables = [jnp.asarray(table) for table in dft_tables(window)]
    vmem = pl.BlockSpec(memory_space=pltpu.VMEM)

    def whole(shape):
        return pl.BlockSpec(shape, lambda i: (0,) * len(shape))

    probe_shape = (slots, 2 * modes * window // slots + 16, window)
    sums_shape = (bands, 4 * (height // bands), window)
    return pl.pallas_call(
        main_kernel,
        grid=(1,),
        out_shape=(
            jax.ShapeDtypeStruct(probe_shape, BF16),
            jax.ShapeDtypeStruct(sums_shape, BF16),
        ),
        in_specs=[
            pl.BlockSpec(memory_space=pltpu.SMEM),
            whole(received.shape),
            pl.BlockSpec((2, height, window), lambda i: (0, 0, 2)),
            whole(margin.shape),
            pl.BlockSpec(memory_space=pltpu.HBM),
        ] + [whole(table.shape) for table in tables],
        out_specs=(whole(probe_shape), whole(sums_shape)),
        scratch_shapes=[
            pltpu.VMEM((slots, 8, window), F32),
            pltpu.VMEM((2, 2, height, window), F32),
            pltpu.VMEM((2, 2, height, window), F32),
            pltpu.VMEM((2 * modes, window, window), F32),
            pltpu.VMEM((modes, 2, window, window), F32),
            pltpu.VMEM((modes, 2, window, window), BF16),
            pltpu.SemaphoreType.DMA,
        ],
        compiler_params=pltpu.CompilerParams(vmem_limit_bytes=40 * 2**20),
    )(notes, received, object_field, margin, probe, *tables)


def exchange(value, axis):
    return lax.all_to_all(value, axis, split_axis=0, concat_axis=0, tiled=True)


def local(object_field, probe, measured, positions):
    tiles = lax.axis_size("tile")
    bands = lax.axis_size("scan")
    width = object_field.shape[2]
    height = object_field.shape[1]
    modes, window = probe.shape[0], probe.shape[2]
    patterns = measured.shape[0]
    deep = height // bands
    piece = 2 * modes * window // tiles
    margin = lax.ppermute(
        object_field[:, :, :window].astype(BF16), "tile", [(t, t - 1) for t in range(1, tiles)]
    )
    received = exchange(pack(positions, measured, tiles), "tile")
    notes = received[:, window, :3].astype(jnp.int32)
    probe_sums, sums = compute(notes, received, object_field, margin, probe, bands)
    mixed = exchange(probe_sums, "tile").astype(F32)
    tile_piece = jnp.sum(mixed[:, :piece], axis=0).astype(BF16)
    everything = exchange(
        jnp.concatenate([sums, jnp.broadcast_to(tile_piece[None], (bands, piece, window))], axis=1),
        "scan",
    )
    gathered = jnp.sum(everything.astype(F32), axis=0)
    full_piece = gathered[4 * deep:] / math.sqrt(patterns * bands * tiles)
    probe_grad = exchange(
        jnp.broadcast_to(full_piece.astype(BF16)[None], (tiles, piece, window)), "tile"
    ).astype(F32).reshape(modes, 2, window, window)
    strips = gathered[:4 * deep].reshape(2, 2, deep, window)
    spilled = lax.ppermute(strips[:, 1], "tile", [(t, t + 1) for t in range(tiles - 1)])
    object_grad = jnp.concatenate(
        [spilled, jnp.zeros((2, deep, width - 2 * window), F32), strips[:, 0]], axis=2
    )
    per_tile = jnp.sum(mixed[:, piece:piece + 2] + mixed[:, piece + 8:piece + 10], axis=2) / window
    left_tile = positions[:, 1] // width
    hits = left_tile[:, None] == jnp.arange(tiles, dtype=jnp.int32)[None, :]
    position_grad = jnp.sum(jnp.where(hits[:, :, None], per_tile[None], 0.0), axis=1)
    return (object_grad, probe_grad, position_grad)


def solution(mesh):
    return jax.shard_map(
        local,
        mesh=mesh,
        in_specs=(
            P(None, None, "tile"),
            P(),
            P(("scan", "tile"), None, None),
            P(("scan", "tile"), None),
        ),
        out_specs=(P(None, "scan", "tile"), P(), P(("scan", "tile"), None)),
        check_vma=False,
    )
```

```python
import math

import jax
import jax.numpy as jnp
import numpy as np
from jax import lax
from jax.experimental import pallas as pl
from jax.experimental.pallas import tpu as pltpu
from jax.sharding import PartitionSpec as P

F32 = jnp.float32
BF16 = jnp.bfloat16
TOP = math.sqrt(12.0)
STEPS = 65535.0
HALF = 32768.0
GROUP = 4
LAG = 1


def dft_tables(window):
    ramp = np.arange(window)
    angles = (ramp[:, None] * ramp[None, :] % window) * (2.0 * np.pi / window)
    cosine = np.cos(angles) / np.sqrt(window)
    sine = np.sin(angles) / np.sqrt(window)
    first = np.block([[cosine, -sine], [sine, cosine]])
    second = np.block([[cosine, sine], [-sine, cosine]])
    tables = []
    for table in (first, second):
        high = table.astype(np.float32).astype(BF16)
        low = (table - high.astype(np.float64)).astype(np.float32).astype(BF16)
        tables += [high, low]
    return [np.stack(tables)]


def split(value):
    high = value.astype(BF16)
    return high, (value - high.astype(F32)).astype(BF16)


def from_right(value, table):
    high = value.astype(BF16)
    return jnp.dot(jnp.concatenate([high, high], axis=1), table, preferred_element_type=F32)


def from_left(table, value):
    high = value.astype(BF16)
    return jnp.dot(table, jnp.concatenate([high, high], axis=0), preferred_element_type=F32)


def pack_kernel(positions, measured, packed, places, loaded, place_sem, load_sems):
    patterns = measured.shape[0]
    slots, rows, window = packed.shape
    place = pltpu.make_async_copy(positions, places, place_sem)
    place.start()
    loads = [
        pltpu.make_async_copy(measured.at[p], loaded.at[p], load_sems.at[p]) for p in range(patterns)
    ]
    for load in loads:
        load.start()
    packed[...] = jnp.zeros(packed.shape, jnp.int16)
    lane = lax.broadcasted_iota(jnp.int32, (rows - window, window), 1)
    place.wait()
    for p in range(patterns):
        row = places[0, p]
        column = places[1, p]
        tile = column // (3 * window)
        start = column - tile * (3 * window) - 2 * window
        note = jnp.where(lane == 0, row, jnp.where(lane == 1, start, jnp.where(lane == 2, 1, 0)))
        packed[tile, window:rows, :] = note.astype(jnp.int16)
        loads[p].wait()
        amplitude = jnp.sqrt(loaded[p]) * (STEPS / TOP)
        level = jnp.clip(jnp.round(amplitude) - HALF, -HALF, HALF - 1.0)
        packed[tile, 0:window, :] = level.astype(jnp.int32).astype(jnp.int16)


def main_kernel(
    notes, received, own, margin, probe, tables,
    probe_sums, patches, shifts, strip, probe_total, probe_full,
    probe_near, probe_sem,
):
    slots = received.shape[0]
    modes = probe.shape[0]
    window = probe.shape[2]
    fetch = pltpu.make_async_copy(probe, probe_near, probe_sem)
    fetch.start()
    for part in range(2):
        strip[part, 0] = own[part].astype(BF16).astype(F32)
        strip[part, 1] = margin[part].astype(F32)
    probe_total[...] = jnp.zeros(probe_total.shape, F32)
    fetch.wait()
    probe_full[...] = probe_near[...].astype(F32)
    lane = lax.broadcasted_iota(jnp.int32, (window, window), 1)
    row = lax.broadcasted_iota(jnp.int32, (window, window), 0)

    def cut(slot):
        start = jnp.clip(notes[slot, 1], 1, window - 1)
        rows = pl.ds(notes[slot, 0], window)
        both = []
        for part in range(2):
            near = pltpu.roll(strip[part, 0, rows, :], window - start, 1)
            far = pltpu.roll(strip[part, 1, rows, :], window - start, 1)
            both.append(jnp.where(lane < window - start, near, far))
        return both

    def leave(w_re, w_im):
        exits = []
        for m in range(modes):
            p_re, p_im = probe_full[m, 0], probe_full[m, 1]
            exits.append(
                jnp.concatenate([p_re * w_re - p_im * w_im, p_re * w_im + p_im * w_re], axis=1)
            )
        return exits

    def scale_of(slot, blocks):
        power = blocks[0][0] * blocks[0][0]
        for m in range(modes):
            for c in range(2):
                if m or c:
                    power = power + blocks[m][c] * blocks[m][c]
        amplitude = (received[slot, 0:window, :].astype(jnp.int32).astype(F32) + HALF) * (TOP / STEPS)
        return notes[slot, 2].astype(F32) * (1.0 - amplitude * lax.rsqrt(jnp.maximum(power, 0.25)))

    def finish(slot, w_re, w_im, back):
        patch_re = jnp.zeros((window, window), F32)
        patch_im = jnp.zeros((window, window), F32)
        for m in range(modes):
            p_re, p_im = probe_full[m, 0], probe_full[m, 1]
            b_re, b_im = back[m]
            patch_re = patch_re + (p_re * b_re + p_im * b_im)
            patch_im = patch_im + (p_re * b_im - p_im * b_re)
            probe_total[2 * m] += w_re * b_re + w_im * b_im
            probe_total[2 * m + 1] += w_re * b_im - w_im * b_re
        for axis, at in ((0, row), (1, lane)):
            change = patch_re * (pltpu.roll(w_re, window - 1, axis) - w_re) + patch_im * (
                pltpu.roll(w_im, window - 1, axis) - w_im
            )
            change = jnp.where(at < window - 1, change, 0.0)
            shifts[slot, pl.ds(axis, 1), :] = jnp.sum(change, axis=0, keepdims=True)
        patches[slot, 0] = patch_re.astype(BF16)
        patches[slot, 1] = patch_im.astype(BF16)

    def joined(at, axis):
        return jnp.concatenate([tables[2 * at], tables[2 * at + 1]], axis=axis)

    def stages(slots_now):
        cuts = [cut(slot) for slot in slots_now]
        exits = [e for w in cuts for e in leave(*w)]
        half = rows_first(exits, joined(0, 0))
        yield
        field = columns_next(half, joined(1, 1))
        yield
        scaled = []
        for u, slot in enumerate(slots_now):
            mine = field[u * modes:(u + 1) * modes]
            scaling = scale_of(slot, mine)
            scaled += [jnp.concatenate([scaling * b[0], scaling * b[1]], axis=1) for b in mine]
        half = rows_first(scaled, joined(1, 0))
        yield
        back = columns_next(half, joined(0, 1))
        yield
        for u, slot in enumerate(slots_now):
            finish(slot, *cuts[u], back[u * modes:(u + 1) * modes])

    def rows_first(blocks, down):
        half = from_right(jnp.concatenate(blocks, axis=0), down)
        return [
            [half[b * window:(b + 1) * window, c * window:(c + 1) * window] for c in range(2)]
            for b in range(len(blocks))
        ]

    def columns_next(pieces, across):
        stacked = jnp.concatenate(
            [jnp.concatenate([p[c] for p in pieces], axis=1) for c in range(2)], axis=0
        )
        out = from_left(across, stacked)
        return [
            [out[c * window:(c + 1) * window, b * window:(b + 1) * window] for c in range(2)]
            for b in range(len(pieces))
        ]

    shifts[...] = jnp.zeros(shifts.shape, F32)
    flows = [stages(range(at, at + GROUP)) for at in range(0, slots, GROUP)]
    for tick in range(5 + LAG * (len(flows) - 1)):
        for at, flow in enumerate(flows):
            if 0 <= tick - LAG * at < 5:
                next(flow, None)
    piece = 2 * modes * window // slots
    for t in range(slots):
        mode, offset = divmod(t * piece, window)
        left, at = piece, 0
        while left:
            take = min(left, window - offset)
            probe_sums[t, at:at + take, :] = probe_total[mode, offset:offset + take, :].astype(BF16)
            mode, offset, left, at = mode + 1, 0, left - take, at + take
        probe_sums[t, piece:, :] = jnp.concatenate(split(shifts[t]), axis=0)


def pack(positions, measured, slots):
    patterns, window = measured.shape[0], measured.shape[2]
    return pl.pallas_call(
        pack_kernel,
        out_shape=jax.ShapeDtypeStruct((slots, window + 16, window), jnp.int16),
        in_specs=[pl.BlockSpec(memory_space=pltpu.HBM)] * 2,
        out_specs=pl.BlockSpec(memory_space=pltpu.VMEM),
        scratch_shapes=[
            pltpu.SMEM((2, patterns), jnp.int32),
            pltpu.VMEM(measured.shape, F32),
            pltpu.SemaphoreType.DMA,
            pltpu.SemaphoreType.DMA((patterns,)),
        ],
        compiler_params=pltpu.CompilerParams(vmem_limit_bytes=60 * 2**20),
    )(positions.T, measured)


def compute(notes, received, object_field, margin, probe):
    modes, window = probe.shape[0], probe.shape[2]
    slots = received.shape[0]
    height = object_field.shape[1]
    tables = [jnp.asarray(table) for table in dft_tables(window)]
    vmem = pl.BlockSpec(memory_space=pltpu.VMEM)

    def whole(shape):
        return pl.BlockSpec(shape, lambda i: (0,) * len(shape))

    probe_shape = (slots, 2 * modes * window // slots + 16, window)
    return pl.pallas_call(
        main_kernel,
        grid=(1,),
        out_shape=(
            jax.ShapeDtypeStruct(probe_shape, BF16),
            jax.ShapeDtypeStruct((slots, 2, window, window), BF16),
        ),
        in_specs=[
            pl.BlockSpec(memory_space=pltpu.SMEM),
            whole(received.shape),
            pl.BlockSpec((2, height, window), lambda i: (0, 0, 2)),
            whole(margin.shape),
            pl.BlockSpec(memory_space=pltpu.HBM),
        ] + [whole(table.shape) for table in tables],
        out_specs=(whole(probe_shape), whole((slots, 2, window, window))),
        scratch_shapes=[
            pltpu.VMEM((slots, 8, window), F32),
            pltpu.VMEM((2, 2, height, window), F32),
            pltpu.VMEM((2 * modes, window, window), F32),
            pltpu.VMEM((modes, 2, window, window), F32),
            pltpu.VMEM((modes, 2, window, window), BF16),
            pltpu.SemaphoreType.DMA,
        ],
        compiler_params=pltpu.CompilerParams(vmem_limit_bytes=59 * 2**20),
    )(notes, received, object_field, margin, probe, *tables)


def deposit_kernel(notes, patches, sums, total):
    slots, window = patches.shape[0], patches.shape[3]
    bands = sums.shape[0]
    deep = sums.shape[1] // 4
    lane = lax.broadcasted_iota(jnp.int32, (window, window), 1)
    total[...] = jnp.zeros(total.shape, F32)
    for slot in range(slots):
        start = jnp.clip(notes[slot, 1], 1, window - 1)
        rows = pl.ds(notes[slot, 0], window)
        for part in range(2):
            turned = pltpu.roll(patches[slot, part].astype(F32), start, 1)
            total[part, 0, rows, :] += jnp.where(lane >= start, turned, 0.0)
            total[part, 1, rows, :] += jnp.where(lane < start, turned, 0.0)
    for b in range(bands):
        for part in range(2):
            for side in range(2):
                at = (2 * part + side) * deep
                sums[b, at:at + deep, :] = total[part, side, b * deep:(b + 1) * deep, :].astype(BF16)


def deposit(notes, patches, bands, height):
    window = patches.shape[3]
    return pl.pallas_call(
        deposit_kernel,
        out_shape=jax.ShapeDtypeStruct((bands, 4 * (height // bands), window), BF16),
        in_specs=[
            pl.BlockSpec(memory_space=pltpu.SMEM),
            pl.BlockSpec(memory_space=pltpu.VMEM),
        ],
        out_specs=pl.BlockSpec(memory_space=pltpu.VMEM),
        scratch_shapes=[pltpu.VMEM((2, 2, height, window), F32)],
        compiler_params=pltpu.CompilerParams(vmem_limit_bytes=16 * 2**20),
        cost_estimate=pl.CostEstimate(flops=4_000_000, bytes_accessed=8_000_000, transcendentals=0),
    )(notes, patches)


def exchange(value, axis):
    return lax.all_to_all(value, axis, split_axis=0, concat_axis=0, tiled=True)


def local(object_field, probe, measured, positions):
    tiles = lax.axis_size("tile")
    bands = lax.axis_size("scan")
    width = object_field.shape[2]
    height = object_field.shape[1]
    modes, window = probe.shape[0], probe.shape[2]
    patterns = measured.shape[0]
    deep = height // bands
    piece = 2 * modes * window // tiles
    margin = lax.ppermute(
        object_field[:, :, :window].astype(BF16), "tile", [(t, t - 1) for t in range(1, tiles)]
    )
    received = exchange(pack(positions, measured, tiles), "tile")
    notes = received[:, window, :3].astype(jnp.int32)
    probe_sums, patches = compute(notes, received, object_field, margin, probe)
    sums = deposit(notes, patches, bands, height)
    mixed = exchange(probe_sums, "tile").astype(F32)
    tile_piece = jnp.sum(mixed[:, :piece], axis=0).astype(BF16)
    everything = exchange(
        jnp.concatenate([sums, jnp.broadcast_to(tile_piece[None], (bands, piece, window))], axis=1),
        "scan",
    )
    gathered = jnp.sum(everything.astype(F32), axis=0)
    full_piece = gathered[4 * deep:] / math.sqrt(patterns * bands * tiles)
    probe_grad = exchange(
        jnp.broadcast_to(full_piece.astype(BF16)[None], (tiles, piece, window)), "tile"
    ).astype(F32).reshape(modes, 2, window, window)
    strips = gathered[:4 * deep].reshape(2, 2, deep, window)
    spilled = lax.ppermute(strips[:, 1], "tile", [(t, t + 1) for t in range(tiles - 1)])
    object_grad = jnp.concatenate(
        [spilled, jnp.zeros((2, deep, width - 2 * window), F32), strips[:, 0]], axis=2
    )
    per_tile = jnp.sum(mixed[:, piece:piece + 2] + mixed[:, piece + 8:piece + 10], axis=2) / window
    left_tile = positions[:, 1] // width
    hits = left_tile[:, None] == jnp.arange(tiles, dtype=jnp.int32)[None, :]
    position_grad = jnp.sum(jnp.where(hits[:, :, None], per_tile[None], 0.0), axis=1)
    return (object_grad, probe_grad, position_grad)


def solution(mesh):
    return jax.shard_map(
        local,
        mesh=mesh,
        in_specs=(
            P(None, None, "tile"),
            P(),
            P(("scan", "tile"), None, None),
            P(("scan", "tile"), None),
        ),
        out_specs=(P(None, "scan", "tile"), P(), P(("scan", "tile"), None)),
        check_vma=False,
    )
```
